32 devices in a mesh: dp: 16 (over z, y, x), tensor: 2 (over core).
Axes of the slice: x: 2, y: 2, z: 4, core: 2. Of those that a mesh axis runs over, the one named last changes fastest.
Arguments:
- residual: bfloat16 [4096, 768], P(('dp', 'tensor')), may hold values from -6 to 6
- cotangent: bfloat16 [4096, 768], P(('dp', 'tensor')), may hold values from -6 to 6
- seq_lengths: int32 [16, 4], P('dp'), may hold values from 0 to 256, as said below
- gain_attn: float32 [768], replicated, may hold values from 0.1 to 1.9
- shift_attn: float32 [768], replicated, may hold values from -1.75 to 1.75
- gain_mlp: float32 [768], replicated, may hold values from 0.1 to 1.9
- shift_mlp: float32 [768], replicated, may hold values from -1.75 to 1.75
- w_qkv: bfloat16 [3, 768, 768], P(None, 'dp', 'tensor'), may hold values from -0.3125 to 0.3125
- b_qkv: float32 [3, 768], P(None, 'tensor'), may hold values from -1.75 to 1.75
- w_out: bfloat16 [768, 768], P('tensor', 'dp'), may hold values from -1.25 to 1.25
- b_out: float32 [768], replicated, may hold values from -1.75 to 1.75
- w_up: bfloat16 [768, 3072], P('dp', 'tensor'), may hold values from -0.21875 to 0.21875
- b_up: float32 [3072], P('tensor'), may hold values from -3 to 3
- w_down: bfloat16 [3072, 768], P('tensor', 'dp'), may hold values from -0.15625 to 0.15625
- b_down: float32 [768], replicated, may hold values from -1.75 to 1.75
Outputs:
- result: bfloat16 [4096, 768], P(('dp', 'tensor'))
- grad_residual: float32 [4096, 768], P(('dp', 'tensor'))
- grad_gain_attn: float32 [768], replicated
- grad_shift_attn: float32 [768], replicated
- grad_gain_mlp: float32 [768], replicated
- grad_shift_mlp: float32 [768], replicated
- grad_w_qkv: float32 [3, 768, 768], P(None, 'dp', 'tensor')
- grad_b_qkv: float32 [3, 768], P(None, 'tensor')
- grad_w_out: float32 [768, 768], P('tensor', 'dp')
- grad_b_out: float32 [768], replicated
- grad_w_up: float32 [768, 3072], P('dp', 'tensor')
- grad_b_up: float32 [3072], P('tensor')
- grad_w_down: float32 [3072, 768], P('tensor', 'dp')
- grad_b_down: float32 [768], replicated
The draws below stay inside these ranges and needn't reach their ends.
Inputs may be any that keep to these rules, and one draw needn't show every extreme that they name: `seq_lengths`: in each group the padded lengths sum to at most 256; the sequence that holds row 127 of a group also holds row 128; in some group a single sequence of exactly 256 rows fills it.
All inputs are finite; a program needn't handle non-finite values.
Results may differ from the reference program's by a relative error of at most 0.012.
The reference program's roundings to bfloat16 on the way count: a program that leaves them out, or rounds other values in their place, can miss the bound.
Values may be sent and summed in bfloat16 or wider, within the bound.
No kernel may reach another device: no remote copies, remote signals or barrier semaphores. Data moves between devices by JAX's collectives and lax.ppermute only.
A program may use at most 128 MiB of HBM per device.

```python
import jax
import jax.numpy as jnp
from jax import lax

D = 768
HEADS = 12
HD = 64
ROT = 16
FF = 3072
SLOTS = 256
BLOCK = 128
NSEQ = 4
GROUPS = 16
TOKENS = 4096


def draw_seq_lengths(key, part):
    key = jax.random.fold_in(key, 11)
    key_used, key_cuts, key_full, key_short = jax.random.split(key, 4)
    blocks = SLOTS // BLOCK
    middle = blocks // 2
    used = jax.random.randint(key_used, (GROUPS,), middle + 1, blocks + 1)
    cuts = jax.random.randint(key_cuts, (GROUPS, NSEQ - 1), 0, blocks + 1)
    cuts = jnp.minimum(cuts, used[:, None])
    cuts = jnp.where(cuts == middle, 0, cuts)
    full_group = jax.random.randint(key_full, (), 0, GROUPS)
    is_full = jnp.arange(GROUPS) == full_group
    used = jnp.where(is_full, blocks, used)
    cuts = jnp.where(is_full[:, None], 0, cuts)
    cuts = jnp.sort(cuts, axis=1)
    bounds = jnp.concatenate([jnp.zeros((GROUPS, 1), jnp.int32), cuts.astype(jnp.int32), used[:, None].astype(jnp.int32)], axis=1)
    counts = bounds[:, 1:] - bounds[:, :-1]
    shortfall = jax.random.randint(key_short, (GROUPS, NSEQ), 0, BLOCK)
    shortfall = jnp.where(is_full[:, None], 0, shortfall)
    return jnp.where(counts > 0, counts * BLOCK - shortfall, 0).astype(jnp.int32)


def shard_levels(stream_key, dims, pieces, low, high):
    def one(axis_at, blocks):
        draws = jax.random.uniform(jax.random.fold_in(jax.random.fold_in(stream_key, 6), axis_at), (blocks,), jnp.float32, low / len(pieces), high / len(pieces))
        return jnp.repeat(jnp.exp(draws), dims[axis_at] // blocks).reshape((-1,) + (1,) * (len(dims) - axis_at - 1))

    level = one(*pieces[0])
    for cut in pieces[1:]:
        level = level * one(*cut)
    return level


def centred(rng, shape, width, reach, cuts=(), kind=jnp.bfloat16):
    drawn = jax.random.normal(rng, shape, jnp.float32) * width
    if len(cuts) > 0:
        drawn = shard_levels(rng, shape, cuts, -0.22, 0.18) * drawn
    return jnp.clip(drawn, min=-reach, max=reach).astype(kind)


def setup_inputs(seed: int = 0) -> dict:
    key_list = jax.random.split(jax.random.key(seed), 16)
    residual = centred(key_list[0], (TOKENS, D), 1.0, 6.0, ((0, 32),))
    cotangent = centred(key_list[1], (TOKENS, D), 1.0, 6.0, ((0, 32),))
    seq_lengths = draw_seq_lengths(jax.random.fold_in(key_list[15], 71), 0)
    gain_attn = jnp.clip(1.0 + 0.18 * jax.random.normal(key_list[3], (D,), jnp.float32), 0.1, 1.9)
    shift_attn = centred(key_list[4], (D,), 0.3, 1.75, (), jnp.float32)
    gain_mlp = jnp.clip(1.0 + 0.18 * jax.random.normal(key_list[5], (D,), jnp.float32), 0.1, 1.9)
    shift_mlp = centred(key_list[6], (D,), 0.3, 1.75, (), jnp.float32)
    w_qkv = centred(key_list[7], (3, D, D), (D // 2) ** -0.5, 0.3125, ((1, 16), (2, 2)))
    b_qkv = centred(key_list[8], (3, D), 0.3, 1.75, ((1, 2),), jnp.float32)
    w_out = centred(key_list[9], (D, D), (D // 32) ** -0.5, 1.25, ((0, 2), (1, 16)))
    b_out = centred(key_list[10], (D,), 0.3, 1.75, (), jnp.float32)
    w_up = centred(key_list[11], (D, FF), D ** -0.5, 0.21875, ((0, 16), (1, 2)))
    b_up = centred(key_list[12], (FF,), 0.5, 3.0, ((0, 2),), jnp.float32)
    w_down = centred(key_list[13], (FF, D), (FF // 2) ** -0.5, 0.15625, ((0, 2), (1, 16)))
    b_down = centred(key_list[14], (D,), 0.3, 1.75, (), jnp.float32)
    return {"residual": residual, "cotangent": cotangent, "seq_lengths": seq_lengths, "gain_attn": gain_attn, "shift_attn": shift_attn, "gain_mlp": gain_mlp, "shift_mlp": shift_mlp, "w_qkv": w_qkv, "b_qkv": b_qkv, "w_out": w_out, "b_out": b_out, "w_up": w_up, "b_up": b_up, "w_down": w_down, "b_down": b_down}


highest = lax.Precision.HIGHEST
eps = 1e-05

@jax.custom_vjp
def low(v):
    return lax.optimization_barrier(v.astype(jnp.bfloat16)).astype(jnp.float32)

@jax.custom_vjp
def low_back(v):
    return v

def low_keep(v):
    return (low(v), None)

def low_pass(kept, grad):
    return (grad,)

def back_keep(v):
    return (v, None)

def back_low(kept, grad):
    return (low(grad),)
low.defvjp(low_keep, low_pass)
low_back.defvjp(back_keep, back_low)

def layout_rows(lengths, row_count, block_rows):
    row_index = jnp.arange(row_count, dtype=jnp.int32)
    padded = ((lengths + block_rows - 1) // block_rows * block_rows).astype(jnp.int32)
    ends = jnp.cumsum(padded).astype(jnp.int32)
    starts = (ends - padded).astype(jnp.int32)
    sequence = lax.optimization_barrier(jnp.sum((row_index[:, None] >= ends[None, :]).astype(jnp.int32), axis=1)).astype(jnp.int32)
    starts_all = jnp.concatenate([starts, ends[-1:]]).astype(jnp.int32)
    lengths_all = jnp.concatenate([lengths.astype(jnp.int32), jnp.zeros((1,), jnp.int32)])
    places = jnp.arange(lengths.shape[0] + 1, dtype=jnp.int32)
    picked = sequence[:, None] == places[None, :]
    first_row = lax.optimization_barrier(jnp.sum(jnp.where(picked, starts_all[None, :], 0), axis=1)).astype(jnp.int32)
    limit = lax.optimization_barrier(jnp.sum(jnp.where(picked, lengths_all[None, :], 0), axis=1)).astype(jnp.int32)
    position = (row_index - first_row).astype(jnp.int32)
    return (sequence, position, position < limit)

def rotate(field, position, rot_dims):
    half = rot_dims // 2
    inverse = 10000.0 ** (-jnp.arange(half, dtype=jnp.float32) * 2.0 / rot_dims)
    angle = position.astype(jnp.float32)[:, None] * inverse[None, :]
    angle = jnp.concatenate([angle, angle], axis=1)
    turned_part = field[..., :rot_dims]
    first_half = turned_part[..., :half]
    second_half = turned_part[..., half:]
    swapped = jnp.concatenate([-second_half, first_half], axis=-1)
    rotated = turned_part * jnp.cos(angle) + swapped * jnp.sin(angle)
    return jnp.concatenate([rotated, field[..., rot_dims:]], axis=-1)

def layer_norm(block_rows, gain, shift):
    centre = lax.optimization_barrier(jnp.mean(block_rows, axis=-1, keepdims=True))
    spread = lax.optimization_barrier(jnp.mean((block_rows - centre) ** 2, axis=-1, keepdims=True))
    return (block_rows - centre) * lax.rsqrt(spread + eps) * gain + shift

def forward(parameters, group_rows, sequence, position, live_row):
    gain_attn, shift_attn, gain_mlp, shift_mlp, w_qkv, b_qkv, w_out, b_out, w_up, b_up, w_down, b_down = parameters
    row_count = group_rows.shape[0]
    first_norm = low(layer_norm(group_rows, gain_attn, shift_attn))
    second_norm = low(layer_norm(group_rows, gain_mlp, shift_mlp))
    projected = low_back(jnp.einsum('sd,cde->cse', first_norm, w_qkv, precision=highest) + b_qkv[:, None, :])
    split_heads = projected.reshape(3, row_count, HEADS, HD).transpose(0, 2, 1, 3)
    queries = low(rotate(split_heads[0], position, ROT))
    key_heads = low(rotate(split_heads[1], position, ROT))
    value_heads = low(split_heads[2])
    logits = low_back(jnp.einsum('hqe,hke->hqk', queries, key_heads, precision=highest) * HD ** (-0.5))
    row_index = jnp.arange(row_count)
    allowed = (sequence[:, None] == sequence[None, :]) & (row_index[None, :] <= row_index[:, None])
    allowed = allowed & (live_row[None, :] | (row_index[None, :] == row_index[:, None]))
    logits = jnp.where(allowed[None], logits, -1000000000.0)
    largest = lax.optimization_barrier(jnp.max(logits, axis=-1, keepdims=True))
    weights = jnp.exp(logits - largest)
    weights = weights / lax.optimization_barrier(jnp.sum(weights, axis=-1, keepdims=True))
    attended = jnp.einsum('hqk,hke->hqe', low(weights), value_heads, precision=highest)
    attended = low(low_back(attended)).transpose(1, 0, 2).reshape(row_count, HEADS * HD)
    attention = jnp.dot(attended, w_out, precision=highest) + b_out
    hidden_pre = low_back(jnp.dot(second_norm, w_up, precision=highest) + b_up)
    activated = low(jax.nn.gelu(hidden_pre, approximate=False))
    feed_out = jnp.dot(activated, w_down, precision=highest) + b_down
    return group_rows + low_back(attention + feed_out)

def reference(residual, cotangent, seq_lengths, gain_attn, shift_attn, gain_mlp, shift_mlp, w_qkv, b_qkv, w_out, b_out, w_up, b_up, w_down, b_down):
    parameters = jax.tree.map(lambda value: value.astype(jnp.float32), (gain_attn, shift_attn, gain_mlp, shift_mlp, w_qkv, b_qkv, w_out, b_out, w_up, b_up, w_down, b_down))
    grouped = residual.astype(jnp.float32).reshape(GROUPS, SLOTS, D)
    grouped_cot = cotangent.astype(jnp.float32).reshape(GROUPS, SLOTS, D)

    def one_group(totals, inputs):
        group_rows, group_cot, lengths = inputs
        sequence, position, live_row = layout_rows(lengths, SLOTS, BLOCK)

        def apply_layer(params_in, rows_in):
            return forward(params_in, rows_in, sequence, position, live_row)
        outcome, pullback = jax.vjp(apply_layer, parameters, group_rows)
        grad_params, grad_rows = pullback(group_cot * live_row[:, None].astype(jnp.float32))
        totals = jax.tree.map(lambda total, extra: total + extra, totals, grad_params)
        return (totals, (outcome, grad_rows))
    zero_totals = jax.tree.map(jnp.zeros_like, parameters)
    totals, (outcomes, grad_rows) = lax.scan(one_group, zero_totals, (grouped, grouped_cot, seq_lengths))
    return (outcomes.reshape(TOKENS, D).astype(jnp.bfloat16), grad_rows.reshape(TOKENS, D), totals[0], totals[1], totals[2], totals[3], totals[4], totals[5], totals[6], totals[7], totals[8], totals[9], totals[10], totals[11])
```

```python
import math
from functools import partial

import jax
import jax.numpy as jnp
from jax import lax
from jax.experimental import pallas as pl
from jax.experimental.pallas import tpu as pltpu
from jax.sharding import PartitionSpec as P

HD = 64
ROT = 16
PLANE = 4
BLK = 2 * HD
NOTES = 16
eps = 1e-05
F32 = jnp.float32
BF16 = jnp.bfloat16


def dot(a, b):
    return jnp.dot(a, b, preferred_element_type=F32)


def dot_nt(a, b):
    return lax.dot_general(a, b, (((1,), (1,)), ((), ())), preferred_element_type=F32)


def dot_tn(a, b):
    return lax.dot_general(a, b, (((0,), (0,)), ((), ())), preferred_element_type=F32)


def xor_sorted(parts, index):
    parts = list(parts)
    bit = 1
    while bit < len(parts):
        swap = (index & bit) != 0
        parts = [jnp.where(swap, parts[j ^ bit], parts[j]) for j in range(len(parts))]
        bit *= 2
    return parts


def tree_sum(parts):
    parts = list(parts)
    while len(parts) > 1:
        parts = [parts[j] + parts[j + 1] for j in range(0, len(parts), 2)]
    return parts[0]


def rotary_tables(rows):
    half = ROT // 2
    inverse = 10000.0 ** (-jnp.arange(half, dtype=F32) * 2.0 / ROT)
    angle = jnp.arange(rows, dtype=F32)[:, None] * inverse[None, :]
    cos, sin = jnp.cos(angle), jnp.sin(angle)
    rest = jnp.ones((rows, HD - ROT), F32)
    none = jnp.zeros((rows, half), F32)
    keep = jnp.concatenate([cos, cos, rest], axis=1)
    low = jnp.concatenate([-sin, none, 0.0 * rest], axis=1)
    high = jnp.concatenate([none, sin, 0.0 * rest], axis=1)
    return tuple(jnp.concatenate([t] * (BLK // HD), axis=1) for t in (keep, low, high))


def rows_kernel(half_ref, length_ref, params_ref, own_ref, peer_ref, x1_ref, x2_ref, xh_ref, g_ref, bo_ref):
    half = half_ref[0]
    own_rows = own_ref.shape[1] // 2
    slots = 2 * own_rows
    params = params_ref[...]
    for k in range(PLANE):
        for which, ref in enumerate((own_ref, peer_ref)):
            part = half if which == 0 else 1 - half
            x = ref[k, :own_rows, :].astype(F32)
            centre = jnp.mean(x, axis=-1, keepdims=True)
            off = x - centre
            spread = jnp.mean(off * off, axis=-1, keepdims=True)
            xh = off * lax.rsqrt(spread + eps)
            at = pl.ds(pl.multiple_of(k * slots + part * own_rows, own_rows), own_rows)
            x1_ref[at, :] = (xh * params[0:1] + params[1:2]).astype(BF16)
            x2_ref[at, :] = (xh * params[2:3] + params[3:4]).astype(BF16)
            xh_ref[at, :] = xh.astype(BF16)
            row = lax.broadcasted_iota(jnp.int32, (own_rows, 1), 0) + part * own_rows
            g = jnp.where(row < length_ref[k], ref[k, own_rows:, :].astype(F32), 0.0)
            g_ref[at, :] = g.astype(BF16)
            if k == 0 and which == 0:
                bo_ref[...] = jnp.sum(g, axis=0, keepdims=True)


def attention_kernel(
    length_ref, x1_ref, g_ref, wa_ref, bias_ref, keep_ref, low_ref, high_ref, att_ref, gp_ref, gw_ref, gb_ref
):
    slots = keep_ref.shape[0]
    keep, low, high = keep_ref[...], low_ref[...], high_ref[...]

    def turn(x, sign):
        return x * keep + sign * (
            pltpu.roll(x, BLK - ROT // 2, 1) * low + pltpu.roll(x, ROT // 2, 1) * high
        )

    lane = lax.broadcasted_iota(jnp.int32, (slots, BLK), 1)
    first = lane < HD
    q_row = lax.broadcasted_iota(jnp.int32, (2 * slots, slots), 0) & (slots - 1)
    k_row = lax.broadcasted_iota(jnp.int32, (2 * slots, slots), 1)

    def stacked(x):
        zero = jnp.zeros_like(x)
        return jnp.concatenate([jnp.where(first, x, zero), jnp.where(first, zero, x)], axis=0)

    def joined(x):
        return jnp.where(first, x[:slots], x[slots:])

    total = jnp.zeros((1, 3 * BLK), F32)
    for k in range(PLANE):
        at = pl.ds(k * slots, slots)
        proj = dot(x1_ref[at, :], wa_ref[:, : 3 * BLK]) + bias_ref[...]
        query = stacked((turn(proj[:, :BLK], 1.0) * HD**-0.5).astype(BF16))
        key = turn(proj[:, BLK : 2 * BLK], 1.0).astype(BF16)
        value = proj[:, 2 * BLK :].astype(BF16)
        ga = stacked(dot(g_ref[at, :], wa_ref[:, 3 * BLK :]).astype(BF16))
        logits = dot_nt(query, key)
        allowed = (k_row <= q_row) & ((k_row < length_ref[k]) | (k_row == q_row))
        logits = jnp.where(allowed, logits, -1000000000.0)
        weights = jnp.exp(logits - jnp.max(logits, axis=-1, keepdims=True))
        probs = weights / jnp.sum(weights, axis=-1, keepdims=True)
        rounded = probs.astype(BF16)
        att_ref[at, :] = joined(dot(rounded, value)).astype(BF16)
        grad_probs = dot_nt(ga, value)
        inner = jnp.sum(probs * grad_probs, axis=-1, keepdims=True)
        grad_logits = (probs * (grad_probs - inner)).astype(BF16)
        grad_query = joined(dot(grad_logits, key)) * HD**-0.5
        grad_key = dot_tn(grad_logits, query)
        grad_value = dot_tn(rounded, ga)
        gp = jnp.concatenate([turn(grad_query, -1.0), turn(grad_key, -1.0), grad_value], axis=1).astype(BF16)
        gp_ref[at, :] = gp
        total = total + jnp.sum(gp.astype(F32), axis=0, keepdims=True)
    gb_ref[...] = total
    gw_ref[:, : 3 * BLK] = dot_tn(x1_ref[...], gp_ref[...]).astype(BF16)
    gw_ref[:, 3 * BLK :] = dot_tn(g_ref[...], att_ref[...]).astype(BF16)


def feed_kernel(
    half_ref, params_ref, x2_ref, xh_ref, g_ref, wf_ref, wa_ref, att_ref, gp_ref, bias_ref, gb_ref, bo_ref,
    keep_ref, send_ref, gw_ref, notes_ref, act_ref, gh_ref, stage_ref
):
    half = half_ref[0]
    own_rows = keep_ref.shape[2]
    slots = 2 * own_rows
    width = bias_ref.shape[1]
    params = params_ref[...]
    gain1, gain2 = params[0:1], params[2:3]
    sums = [jnp.zeros((1, x2_ref.shape[1]), F32) for _ in range(4)]
    gb_up = jnp.zeros((1, width), F32)
    for k in range(PLANE):
        at = pl.ds(k * slots, slots)
        hidden = dot(x2_ref[at, :], wf_ref[:, :width]) + bias_ref[...]
        grad_act = dot(g_ref[at, :], wf_ref[:, width:])
        part = 0.5 + 0.5 * lax.erf(hidden * (0.5**0.5))
        act = (hidden * part).astype(BF16)
        slope = part + hidden * jnp.exp(-0.5 * hidden * hidden) * (2.0 * math.pi) ** -0.5
        gh = (grad_act * slope).astype(BF16)
        act_ref[at, :] = act
        gh_ref[at, :] = gh
        gb_up = gb_up + jnp.sum(gh.astype(F32), axis=0, keepdims=True)
        stage_ref[0] = dot_nt(act, wf_ref[:, width:]) + dot_nt(att_ref[at, :], wa_ref[:, 3 * BLK :])
        g1 = dot_nt(gp_ref[at, :], wa_ref[:, : 3 * BLK])
        g2 = dot_nt(gh, wf_ref[:, :width])
        stage_ref[1] = gain1 * g1 + gain2 * g2
        xh = xh_ref[at, :].astype(F32)
        for j, term in enumerate((g1 * xh, g1, g2 * xh, g2)):
            sums[j] = sums[j] + jnp.sum(term, axis=0, keepdims=True)
        mine = pl.ds(pl.multiple_of(half * own_rows, own_rows), own_rows)
        other = pl.ds(pl.multiple_of((1 - half) * own_rows, own_rows), own_rows)
        for j in range(2):
            keep_ref[j, k] = stage_ref[j, mine, :].astype(BF16)
            send_ref[j, k] = stage_ref[j, other, :].astype(BF16)
    gw_ref[:, :width] = dot_tn(x2_ref[...], gh_ref[...]).astype(BF16)
    gw_ref[:, width:] = dot_tn(g_ref[...], act_ref[...]).astype(BF16)
    notes_ref[...] = jnp.zeros_like(notes_ref)
    notes_ref[0:1, :width] = gb_up
    notes_ref[0:1, width:] = gb_ref[...]
    notes_ref[1:2, :] = bo_ref[...]
    for j in range(4):
        notes_ref[2 + j : 3 + j, :] = sums[j]


def kernel_call(body, out_shapes, in_smem, operands, scratch=(), flops=0):
    vmem = pl.BlockSpec(memory_space=pltpu.VMEM)
    smem = pl.BlockSpec(memory_space=pltpu.SMEM)
    bytes_accessed = sum(
        math.prod(a.shape) * a.dtype.itemsize for a in list(operands) + list(out_shapes)
    )
    return pl.pallas_call(
        body,
        out_shape=out_shapes,
        in_specs=[smem] * in_smem + [vmem] * (len(operands) - in_smem),
        out_specs=[vmem] * len(out_shapes),
        scratch_shapes=list(scratch),
        compiler_params=pltpu.CompilerParams(vmem_limit_bytes=48 * 2**20),
        cost_estimate=pl.CostEstimate(flops=flops, bytes_accessed=bytes_accessed, transcendentals=0),
    )(*operands)


def per_device(
    residual,
    cotangent,
    seq_lengths,
    gain_attn,
    shift_attn,
    gain_mlp,
    shift_mlp,
    w_qkv,
    b_qkv,
    w_out,
    b_out,
    w_up,
    b_up,
    w_down,
    b_down,
):
    places = lax.axis_size("dp")
    levels = places // PLANE
    index = lax.axis_index("dp")
    half = lax.axis_index("tensor")
    plane_at = index % PLANE
    level_at = index // PLANE
    own_rows, model = residual.shape
    slots = 2 * own_rows
    owned = w_up.shape[0]
    width = w_up.shape[1] // PLANE
    head_blocks = w_out.shape[0] // BLK
    direct = levels <= 4
    level_groups = [[lev * PLANE + j for lev in range(levels)] for j in range(PLANE)]

    def to_plane(x, k):
        return lax.ppermute(x, "dp", [(j, j ^ k) for j in range(places)])

    def to_level(x, m):
        return lax.ppermute(x, "dp", [(j, j ^ (m * PLANE)) for j in range(places)])

    def to_peer(x):
        return lax.ppermute(x, "tensor", [(0, 1), (1, 0)])

    def gather_levels(x):
        if direct:
            return xor_sorted([x] + [to_level(x, m) for m in range(1, levels)], level_at)
        every = lax.all_gather(x, "dp", axis=0, axis_index_groups=level_groups)
        return [every[j] for j in range(levels)]

    def scatter_levels(x, notes):
        chunk = model // levels
        if direct:
            def message(m):
                rows = lax.dynamic_slice_in_dim(x, (level_at ^ m) * chunk, chunk, 0)
                return rows if notes is None else jnp.concatenate([rows, notes], axis=0)

            parts = [message(0)] + [to_level(message(m), m) for m in range(1, levels)]
            total = tree_sum([part.astype(F32) for part in parts])
            return total[:chunk], total[chunk:]
        rows = lax.psum_scatter(x, "dp", scatter_dimension=0, tiled=True, axis_index_groups=level_groups)
        if notes is not None:
            every = lax.all_gather(notes, "dp", axis=0, axis_index_groups=level_groups)
            notes = jnp.sum(every.astype(F32), axis=0)
        return rows.astype(F32), notes

    def share(place):
        at = jnp.minimum(place, head_blocks - 1) * BLK
        qkv = lax.dynamic_slice_in_dim(w_qkv, at, BLK, 2)
        out = lax.dynamic_slice_in_dim(w_out, at, BLK, 0).T
        heads = jnp.concatenate([qkv[0], qkv[1], qkv[2], out], axis=1)
        heads = jnp.where(place < head_blocks, heads, jnp.zeros_like(heads))
        up = lax.dynamic_slice_in_dim(w_up, place * width, width, 1)
        down = lax.dynamic_slice_in_dim(w_down, place * width, width, 0).T
        return jnp.concatenate([heads, up, down], axis=1)

    shares = [share(plane_at)] + [to_plane(share(plane_at ^ k), k) for k in range(1, PLANE)]
    shares = jnp.concatenate(xor_sorted(shares, plane_at), axis=0)

    length = jnp.sum(seq_lengths[0])
    lengths_rows = jnp.full((NOTES, model), length.astype(BF16))
    message = jnp.concatenate([residual, cotangent, lengths_rows], axis=0)
    messages = [message] + [to_plane(message, k) for k in range(1, PLANE)]
    lengths = jnp.stack([part[slots, 0] for part in messages]).astype(jnp.int32)
    own = jnp.stack([part[:slots] for part in messages])
    peer = to_peer(own)

    wa = jnp.concatenate(gather_levels(shares[:, : 4 * BLK]), axis=0)
    wf = jnp.concatenate(gather_levels(shares[:, 4 * BLK :]), axis=0)

    half_s = half.astype(jnp.int32).reshape(1)
    params = jnp.stack([gain_attn, shift_attn, gain_mlp, shift_mlp] + [jnp.zeros_like(gain_attn)] * 4)
    rows_all = PLANE * slots
    shape = jax.ShapeDtypeStruct
    x1, x2, xh, g, bo = kernel_call(
        rows_kernel,
        [shape((rows_all, model), BF16)] * 4 + [shape((1, model), F32)],
        2,
        (half_s, lengths, params, own, peer),
        flops=rows_all * model * 20,
    )

    block_at = jnp.minimum(plane_at, head_blocks - 1) * BLK
    bias_heads = lax.dynamic_slice_in_dim(b_qkv, block_at, BLK, 1).reshape(1, 3 * BLK)
    att, gp, gw_heads, gb = kernel_call(
        attention_kernel,
        [
            shape((rows_all, BLK), BF16),
            shape((rows_all, 3 * BLK), BF16),
            shape((model, 4 * BLK), BF16),
            shape((1, 3 * BLK), F32),
        ],
        1,
        (lengths, x1, g, wa, bias_heads) + rotary_tables(slots),
        flops=4 * rows_all * model * 4 * BLK + 12 * rows_all * 2 * slots * BLK,
    )
    grad_heads, _ = scatter_levels(gw_heads, None)

    bias_up = lax.dynamic_slice_in_dim(b_up, plane_at * width, width, 0).reshape(1, width)
    keep, send, gw_feed, notes = kernel_call(
        feed_kernel,
        [
            shape((2, PLANE, own_rows, model), BF16),
            shape((2, PLANE, own_rows, model), BF16),
            shape((model, 2 * width), BF16),
            shape((NOTES, model), F32),
        ],
        1,
        (half_s, params, x2, xh, g, wf, wa, att, gp, bias_up, gb, bo),
        scratch=[
            pltpu.VMEM((rows_all, width), BF16),
            pltpu.VMEM((rows_all, width), BF16),
            pltpu.VMEM((2, slots, model), F32),
        ],
        flops=12 * rows_all * model * width,
    )
    grad_feed, notes = scatter_levels(gw_feed, notes.astype(BF16))

    summed = (keep.astype(F32) + to_peer(send).astype(F32)).astype(BF16)
    parts = [summed[:, 0]] + [to_plane(summed[:, k], k) for k in range(1, PLANE)]
    branch, grad_norm = tree_sum([part.astype(F32) for part in parts])
    residual_f = residual.astype(F32)
    result = (residual_f + (branch + b_out + b_down)).astype(BF16)
    centre = jnp.mean(residual_f, axis=-1, keepdims=True)
    off = residual_f - centre
    scale = lax.rsqrt(jnp.mean(off * off, axis=-1, keepdims=True) + eps)
    xh_own = off * scale
    row = half * own_rows + jnp.arange(own_rows, dtype=jnp.int32)
    grad_out = jnp.where((row < length)[:, None], cotangent.astype(F32), 0.0)
    grad_residual = grad_out + scale * (
        grad_norm
        - jnp.mean(grad_norm, axis=-1, keepdims=True)
        - xh_own * jnp.mean(grad_norm * xh_own, axis=-1, keepdims=True)
    )

    grad_heads = grad_heads.astype(BF16).reshape(PLANE, owned, 4 * BLK)
    grad_feed = grad_feed.astype(BF16).reshape(PLANE, owned, 2 * width)
    notes = notes.astype(BF16)

    def back(place):
        feed = lax.dynamic_index_in_dim(grad_feed, place, 0, keepdims=False)
        heads = lax.dynamic_index_in_dim(grad_heads, place, 0, keepdims=False)
        return jnp.concatenate([feed, notes], axis=0), heads

    feeds, heads = [], []
    for k in range(PLANE):
        feed, head = back(plane_at ^ k)
        feeds.append(feed if k == 0 else to_plane(feed, k))
        heads.append(head if k == 0 else to_plane(head, k))
    common = tree_sum([part[owned + 1 : owned + 6].astype(F32) for part in feeds])
    common = common + to_peer(common)
    feeds = [part.astype(F32) for part in xor_sorted(feeds, plane_at)]
    heads = [part.astype(F32) for part in xor_sorted(heads, plane_at)][:head_blocks]
    grad_up = jnp.concatenate([part[:owned, :width] for part in feeds], axis=1)
    grad_down = jnp.concatenate([part[:owned, width:] for part in feeds], axis=1).T
    grad_qkv = jnp.stack(
        [jnp.concatenate([part[:, c * BLK : (c + 1) * BLK] for part in heads], axis=1) for c in range(3)]
    )
    grad_out_w = jnp.concatenate([part[:, 3 * BLK :] for part in heads], axis=1).T
    grad_b_up = jnp.concatenate([part[owned, :width] for part in feeds])
    grad_b_qkv = jnp.concatenate(
        [part[owned, width:].reshape(3, BLK) for part in feeds[:head_blocks]], axis=1
    )
    return (
        result,
        grad_residual,
        common[1],
        common[2],
        common[3],
        common[4],
        grad_qkv,
        grad_b_qkv,
        grad_out_w,
        common[0],
        grad_up,
        grad_b_up,
        grad_down,
        common[0],
    )


def solution(mesh):
    return jax.shard_map(
        per_device,
        mesh=mesh,
        in_specs=(
            P(("dp", "tensor"), None),
            P(("dp", "tensor"), None),
            P("dp", None),
            P(),
            P(),
            P(),
            P(),
            P(None, "dp", "tensor"),
            P(None, "tensor"),
            P("tensor", "dp"),
            P(),
            P("dp", "tensor"),
            P("tensor"),
            P("tensor", "dp"),
            P(),
        ),
        out_specs=(
            P(("dp", "tensor"), None),
            P(("dp", "tensor"), None),
            P(),
            P(),
            P(),
            P(),
            P(None, "dp", "tensor"),
            P(None, "tensor"),
            P("tensor", "dp"),
            P(),
            P("dp", "tensor"),
            P("tensor"),
            P("tensor", "dp"),
            P(),
        ),
        check_vma=False,
    )
```

```python
import math
from functools import partial

import jax
import jax.numpy as jnp
import numpy as np
from jax import lax
from jax.experimental import pallas as pl
from jax.experimental.pallas import tpu as pltpu
from jax.sharding import PartitionSpec as P

HD = 64
ROT = 16
PLANE = 4
BLK = 2 * HD
NOTES = 16
eps = 1e-05
F32 = jnp.float32
BF16 = jnp.bfloat16


def dot(a, b):
    return jnp.dot(a, b, preferred_element_type=F32)


def dot_nt(a, b):
    return lax.dot_general(a, b, (((1,), (1,)), ((), ())), preferred_element_type=F32)


def dot_tn(a, b):
    return lax.dot_general(a, b, (((0,), (0,)), ((), ())), preferred_element_type=F32)


def xor_sorted(parts, index):
    parts = list(parts)
    bit = 1
    while bit < len(parts):
        swap = (index & bit) != 0
        parts = [jnp.where(swap, parts[j ^ bit], parts[j]) for j in range(len(parts))]
        bit *= 2
    return parts


def tree_sum(parts):
    parts = list(parts)
    while len(parts) > 1:
        parts = [parts[j] + parts[j + 1] for j in range(0, len(parts), 2)]
    return parts[0]


def rotary_tables(rows):
    half = ROT // 2
    inverse = np.float32(10000.0) ** (-np.arange(half, dtype=np.float32) * np.float32(2.0 / ROT))
    angle = np.arange(rows, dtype=np.float32)[:, None] * inverse.astype(np.float32)[None, :]
    cos, sin = np.cos(angle), np.sin(angle)
    rest = np.ones((rows, HD - ROT), np.float32)
    none = np.zeros((rows, half), np.float32)
    keep = np.concatenate([cos, cos, rest], axis=1)
    low = np.concatenate([-sin, none, 0.0 * rest], axis=1)
    high = np.concatenate([none, sin, 0.0 * rest], axis=1)
    return tuple(
        np.concatenate([t] * (BLK // HD), axis=1).astype(np.float32) for t in (keep, low, high)
    )


def share_kernel(place_ref, qkv_ref, out_ref, up_ref, down_ref, *share_refs):
    head_blocks = out_ref.shape[1] // BLK
    width = up_ref.shape[1] // PLANE
    for k in range(PLANE):
        place = place_ref[0] ^ k
        at = pl.ds(pl.multiple_of(jnp.minimum(place, head_blocks - 1) * BLK, BLK), BLK)
        for c in range(4):
            block = qkv_ref[c, :, at] if c < 3 else out_ref[:, at]
            block = jnp.where(place < head_blocks, block.astype(F32), 0.0)
            share_refs[k][:, c * BLK : (c + 1) * BLK] = block.astype(BF16)
        at = pl.ds(pl.multiple_of(place * width, BLK), width)
        share_refs[k][:, 4 * BLK : 4 * BLK + width] = up_ref[:, at]
        share_refs[k][:, 4 * BLK + width :] = down_ref[:, at]


def place_rows(place_ref, piece_refs, to_ref):
    plane_at, level_at = place_ref[0], place_ref[1]
    owned = piece_refs[0].shape[0] // PLANE
    for m, piece_ref in enumerate(piece_refs):
        for k in range(PLANE):
            at = ((level_at ^ m) * PLANE + (plane_at ^ k)) * owned
            to_ref[pl.ds(pl.multiple_of(at, owned), owned), :] = piece_ref[k * owned : (k + 1) * owned, :]


def take_rows(place_ref, from_ref, m, k, owned):
    at = ((place_ref[1] ^ m) * PLANE + (place_ref[0] ^ k)) * owned
    return from_ref[pl.ds(pl.multiple_of(at, owned), owned), :]


def rows_kernel(half_ref, params_ref, *refs):
    own_refs, peer_refs = refs[:2], refs[2:4]
    x1_ref, x2_ref, xh_ref, g_ref, g_own_ref, length_ref, bo_ref = refs[4:]
    half = half_ref[0]
    own_rows = g_own_ref.shape[0]
    slots = 2 * own_rows
    message_rows = own_refs[0].shape[0] // 2
    params = params_ref[...]
    length_ref[...] = jnp.zeros_like(length_ref)
    for k in range(PLANE):
        start = (k % 2) * message_rows
        length = own_refs[k // 2][start + slots : start + slots + NOTES, :].astype(F32)
        length = jnp.sum(length[0:1], axis=-1, keepdims=True)
        length_ref[k : k + 1, :] = jnp.broadcast_to(length, (1, length_ref.shape[1]))
        for which, parts in enumerate((own_refs, peer_refs)):
            part = half if which == 0 else 1 - half
            ref = parts[k // 2]
            x = ref[start : start + own_rows, :].astype(F32)
            centre = jnp.mean(x, axis=-1, keepdims=True)
            off = x - centre
            spread = jnp.mean(off * off, axis=-1, keepdims=True)
            xh = off * lax.rsqrt(spread + eps)
            at = pl.ds(pl.multiple_of(k * slots + part * own_rows, own_rows), own_rows)
            x1_ref[at, :] = (xh * params[0:1] + params[1:2]).astype(BF16)
            x2_ref[at, :] = (xh * params[2:3] + params[3:4]).astype(BF16)
            xh_ref[at, :] = xh.astype(BF16)
            row = lax.broadcasted_iota(jnp.int32, (own_rows, 1), 0) + part * own_rows
            g = ref[start + own_rows : start + slots, :].astype(F32)
            g = jnp.where(row.astype(F32) < length, g, 0.0)
            g_ref[at, :] = g.astype(BF16)
            if k == 0 and which == 0:
                g_own_ref[...] = g.astype(BF16)
                bo_ref[...] = jnp.sum(g, axis=0, keepdims=True)


def attention_kernel(levels, *refs):
    place_ref, length_ref, x1_ref, g_ref, bias_ref, keep_ref, low_ref, high_ref = refs[:8]
    pieces = refs[8 : 8 + max(levels, 1)]
    att_ref, gp_ref, wa_ref, gb_ref = refs[8 + len(pieces) : 12 + len(pieces)]
    message_refs, gw_ref = refs[12 + len(pieces) : -1], refs[-1]
    if levels:
        place_rows(place_ref, pieces, wa_ref)
    else:
        wa_ref[...] = pieces[0][...]
        gw_ref = message_refs[0]
    slots = keep_ref.shape[0]
    keep, low, high = keep_ref[...], low_ref[...], high_ref[...]

    def turn(x, sign):
        return x * keep + sign * (
            pltpu.roll(x, BLK - ROT // 2, 1) * low + pltpu.roll(x, ROT // 2, 1) * high
        )

    lane = lax.broadcasted_iota(jnp.int32, (slots, BLK), 1)
    first = lane < HD
    q_row = lax.broadcasted_iota(jnp.int32, (2 * slots, slots), 0) & (slots - 1)
    k_row = lax.broadcasted_iota(jnp.int32, (2 * slots, slots), 1)

    def stacked(x):
        zero = jnp.zeros_like(x)
        return jnp.concatenate([jnp.where(first, x, zero), jnp.where(first, zero, x)], axis=0)

    def joined(x):
        return jnp.where(first, x[:slots], x[slots:])

    total = jnp.zeros((1, 3 * BLK), F32)
    for k in range(PLANE):
        at = pl.ds(k * slots, slots)
        proj = dot(x1_ref[at, :], wa_ref[:, : 3 * BLK]) + bias_ref[...]
        query = stacked((turn(proj[:, :BLK], 1.0) * HD**-0.5).astype(BF16))
        key = turn(proj[:, BLK : 2 * BLK], 1.0).astype(BF16)
        value = proj[:, 2 * BLK :].astype(BF16)
        ga = stacked(dot(g_ref[at, :], wa_ref[:, 3 * BLK :]).astype(BF16))
        logits = dot_nt(query, key)
        live = k_row.astype(F32) < length_ref[k : k + 1, 0:1]
        allowed = (k_row <= q_row) & (live | (k_row == q_row))
        logits = jnp.where(allowed, logits, -1000000000.0)
        weights = jnp.exp(logits - jnp.max(logits, axis=-1, keepdims=True))
        probs = weights / jnp.sum(weights, axis=-1, keepdims=True)
        rounded = probs.astype(BF16)
        att_ref[at, :] = joined(dot(rounded, value)).astype(BF16)
        grad_probs = dot_nt(ga, value)
        inner = jnp.sum(probs * grad_probs, axis=-1, keepdims=True)
        grad_logits = (probs * (grad_probs - inner)).astype(BF16)
        grad_query = joined(dot(grad_logits, key)) * HD**-0.5
        grad_key = dot_tn(grad_logits, query)
        grad_value = dot_tn(rounded, ga)
        gp = jnp.concatenate([turn(grad_query, -1.0), turn(grad_key, -1.0), grad_value], axis=1).astype(BF16)
        gp_ref[at, :] = gp
        total = total + jnp.sum(gp.astype(F32), axis=0, keepdims=True)
    gb_ref[...] = total
    gw_ref[:, : 3 * BLK] = dot_tn(x1_ref[...], gp_ref[...]).astype(BF16)
    gw_ref[:, 3 * BLK :] = dot_tn(g_ref[...], att_ref[...]).astype(BF16)
    if levels:
        owned = pieces[0].shape[0] // PLANE
        for m in range(levels):
            for k in range(PLANE):
                message_refs[m][k * owned : (k + 1) * owned, :] = take_rows(place_ref, gw_ref, m, k, owned)


def feed_kernel(levels, *refs):
    place_ref, half_ref, params_ref, x2_ref, xh_ref, g_ref, wa_ref, att_ref, gp_ref = refs[:9]
    bias_ref, gb_ref, bo_ref = refs[9:12]
    pieces = refs[12 : 12 + max(levels, 1)]
    keep_ref, send_ref, notes_ref = refs[12 + len(pieces) : 15 + len(pieces)]
    message_refs = refs[15 + len(pieces) : -5]
    wf_ref, gw_ref, act_ref, gh_ref, stage_ref = refs[-5:]
    width = bias_ref.shape[1]
    if levels:
        place_rows(place_ref, pieces, wf_ref)
    else:
        wf_ref[...] = pieces[0][...]
        gw_ref = message_refs[0]
    half = half_ref[0]
    own_rows = keep_ref.shape[2]
    slots = 2 * own_rows
    params = params_ref[...]
    gain1, gain2 = params[0:1], params[2:3]
    sums = [jnp.zeros((1, x2_ref.shape[1]), F32) for _ in range(4)]
    gb_up = jnp.zeros((1, width), F32)
    for k in range(PLANE):
        at = pl.ds(k * slots, slots)
        hidden = dot(x2_ref[at, :], wf_ref[:, :width]) + bias_ref[...]
        grad_act = dot(g_ref[at, :], wf_ref[:, width:])
        part = 0.5 + 0.5 * lax.erf(hidden * (0.5**0.5))
        act = (hidden * part).astype(BF16)
        slope = part + hidden * jnp.exp(-0.5 * hidden * hidden) * (2.0 * math.pi) ** -0.5
        gh = (grad_act * slope).astype(BF16)
        act_ref[at, :] = act
        gh_ref[at, :] = gh
        gb_up = gb_up + jnp.sum(gh.astype(F32), axis=0, keepdims=True)
        stage_ref[0] = dot_nt(act, wf_ref[:, width:]) + dot_nt(att_ref[at, :], wa_ref[:, 3 * BLK :])
        g1 = dot_nt(gp_ref[at, :], wa_ref[:, : 3 * BLK])
        g2 = dot_nt(gh, wf_ref[:, :width])
        stage_ref[1] = gain1 * g1 + gain2 * g2
        xh = xh_ref[at, :].astype(F32)
        for j, term in enumerate((g1 * xh, g1, g2 * xh, g2)):
            sums[j] = sums[j] + jnp.sum(term, axis=0, keepdims=True)
        mine = pl.ds(pl.multiple_of(half * own_rows, own_rows), own_rows)
        other = pl.ds(pl.multiple_of((1 - half) * own_rows, own_rows), own_rows)
        for j in range(2):
            keep_ref[j, k] = stage_ref[j, mine, :].astype(BF16)
            send_ref[j, k] = stage_ref[j, other, :].astype(BF16)
    gw_ref[:, :width] = dot_tn(x2_ref[...], gh_ref[...]).astype(BF16)
    gw_ref[:, width:] = dot_tn(g_ref[...], act_ref[...]).astype(BF16)
    notes_ref[...] = jnp.zeros_like(notes_ref)
    notes_ref[0:1, :width] = gb_up
    notes_ref[0:1, width:] = gb_ref[...]
    notes_ref[1:2, :] = bo_ref[...]
    for j in range(4):
        notes_ref[2 + j : 3 + j, :] = sums[j]
    if levels:
        owned = pieces[0].shape[0] // PLANE
        notes = notes_ref[...].astype(BF16)
        for m in range(levels):
            for k in range(PLANE):
                message_refs[m][k * owned : (k + 1) * owned, :] = take_rows(place_ref, gw_ref, m, k, owned)
            message_refs[m][PLANE * owned :, :] = notes


def combine_kernel(inner_ref, *refs):
    head_refs, feed_refs, out_refs = refs[:4], refs[4:8], refs[8:]
    owned = head_refs[0].shape[0] // PLANE
    head_columns = head_refs[0].shape[1]
    inner = inner_ref[0] != 0

    def summed(refs, rows):
        own, near, middle, far = [ref[rows, :].astype(F32) for ref in refs]
        return (own + near) + (jnp.where(inner, 0.0, middle) + far)

    at = pl.ds(PLANE * owned, NOTES)
    own, near, middle, far = [ref[at, :].astype(F32) for ref in feed_refs]
    passed = feed_refs[3][PLANE * owned + NOTES :, :].astype(F32)
    notes = ((own + near) + (jnp.where(inner, passed, middle) + far)).astype(BF16)
    for k, out_ref in enumerate(out_refs):
        rows = pl.ds(k * owned, owned)
        out_ref[:owned, :head_columns] = summed(head_refs, rows).astype(out_ref.dtype)
        out_ref[:owned, head_columns:] = summed(feed_refs, rows).astype(out_ref.dtype)
        out_ref[owned:, :head_columns] = jnp.zeros((NOTES, head_columns), out_ref.dtype)
        out_ref[owned:, head_columns:] = notes.astype(out_ref.dtype)


def owner_kernel(place_ref, *refs):
    part_refs = refs[:PLANE]
    up_ref, down_ref, qkv_ref, out_ref, b_up_ref, b_qkv_ref, common_ref = refs[PLANE:]
    owned = up_ref.shape[0]
    width = up_ref.shape[1] // PLANE
    head_blocks = out_ref.shape[1] // BLK
    start = 4 * BLK
    for k, part_ref in enumerate(part_refs):
        place = place_ref[0] ^ k
        at = pl.ds(pl.multiple_of(place * width, BLK), width)
        up_ref[:, at] = part_ref[:owned, start : start + width].astype(F32)
        down_ref[:, at] = part_ref[:owned, start + width :].astype(F32)
        notes = part_ref[owned:, start:].astype(F32)
        b_up_ref[:, at] = notes[0:1, :width]

        @pl.when(place < head_blocks)
        def _():
            at = pl.ds(pl.multiple_of(place * BLK, BLK), BLK)
            for c in range(3):
                qkv_ref[c, :, at] = part_ref[:owned, c * BLK : (c + 1) * BLK].astype(F32)
                b_qkv_ref[c : c + 1, at] = notes[0:1, width + c * BLK : width + (c + 1) * BLK]
            out_ref[:, at] = part_ref[:owned, 3 * BLK : 4 * BLK].astype(F32)

    common_ref[...] = tree_sum([part_ref[owned:, start:].astype(F32) for part_ref in part_refs])


def kernel_call(body, out_shapes, in_smem, operands, scratch=(), micros=1.0):
    vmem = pl.BlockSpec(memory_space=pltpu.VMEM)
    smem = pl.BlockSpec(memory_space=pltpu.SMEM)
    return pl.pallas_call(
        body,
        out_shape=out_shapes,
        in_specs=[smem] * in_smem + [vmem] * (len(operands) - in_smem),
        out_specs=[vmem] * len(out_shapes),
        scratch_shapes=list(scratch),
        compiler_params=pltpu.CompilerParams(vmem_limit_bytes=48 * 2**20),
        cost_estimate=pl.CostEstimate(flops=int(micros * 1e9), bytes_accessed=1, transcendentals=0),
    )(*operands)


def per_device(
    residual,
    cotangent,
    seq_lengths,
    gain_attn,
    shift_attn,
    gain_mlp,
    shift_mlp,
    w_qkv,
    b_qkv,
    w_out,
    b_out,
    w_up,
    b_up,
    w_down,
    b_down,
):
    places = lax.axis_size("dp")
    levels = places // PLANE
    index = lax.axis_index("dp")
    half = lax.axis_index("tensor")
    plane_at = index % PLANE
    level_at = index // PLANE
    own_rows, model = residual.shape
    slots = 2 * own_rows
    rows_all = PLANE * slots
    owned = w_up.shape[0]
    width = w_up.shape[1] // PLANE
    head_blocks = w_out.shape[0] // BLK
    direct = levels if levels == 4 and owned % 16 == 0 else 0
    level_groups = [[lev * PLANE + j for lev in range(levels)] for j in range(PLANE)]
    shape = jax.ShapeDtypeStruct

    def to_plane(x, k):
        return lax.ppermute(x, "dp", [(j, j ^ k) for j in range(places)])

    def to_level(x, m):
        return lax.ppermute(x, "dp", [(j, j ^ (m * PLANE)) for j in range(places)])

    def to_peer(x):
        return lax.ppermute(x, "tensor", [(0, 1), (1, 0)])

    inner = (level_at == 1) | (level_at == 2)
    passing = [(0, 2), (3, 1), (1, 0), (2, 3)]

    def to_pass(x, back=False):
        pairs = [(b, a) if back else (a, b) for a, b in passing]
        return lax.ppermute(x, "dp", [(a * PLANE + j, b * PLANE + j) for a, b in pairs for j in range(PLANE)])

    def gather_line(x):
        near, far = to_level(x, 1), to_level(x, 3)
        return near, far, to_pass(jnp.where(inner, far, x))

    place_s = jnp.stack([plane_at, level_at]).astype(jnp.int32)
    half_s = half.astype(jnp.int32).reshape(1)

    shares = kernel_call(
        share_kernel,
        [shape((owned, 4 * BLK + 2 * width), BF16)] * PLANE,
        1,
        (place_s, w_qkv, w_out.T, w_up, w_down.T),
    )
    received = [to_plane(shares[k], k) for k in range(1, PLANE)]
    if direct:
        every = jnp.concatenate([shares[0]] + received, axis=0)
        head_own, feed_own = every[:, : 4 * BLK], every[:, 4 * BLK :]
        near, far, middle = gather_line(head_own)
        head_pieces = [head_own, near, middle, far]
        feed_own, _ = lax.optimization_barrier((feed_own, far))
        near, far, middle = gather_line(feed_own)
        feed_pieces = [feed_own, near, middle, far]
    else:
        every = jnp.concatenate(xor_sorted([shares[0]] + received, plane_at), axis=0)
        every = lax.all_gather(every, "dp", axis=0, tiled=True, axis_index_groups=level_groups)
        head_pieces, feed_pieces = [every[:, : 4 * BLK]], [every[:, 4 * BLK :]]

    notes = jnp.pad(seq_lengths.astype(BF16), ((0, NOTES - 1), (0, model - seq_lengths.shape[1])))
    message = jnp.concatenate([residual, cotangent, notes], axis=0)
    message, _ = lax.optimization_barrier((message, shares))
    pair = jnp.concatenate([message, to_plane(message, 1)], axis=0)
    other_pair = to_plane(pair, 2)
    peers = to_peer(pair), to_peer(other_pair)

    params = jnp.stack([gain_attn, shift_attn, gain_mlp, shift_mlp] + [jnp.zeros_like(gain_attn)] * 4)
    x1, x2, xh, g, g_own, lengths, bo = kernel_call(
        rows_kernel,
        [shape((rows_all, model), BF16)] * 4
        + [shape((own_rows, model), BF16), shape((8, 128), F32), shape((1, model), F32)],
        1,
        (half_s, params, pair, other_pair, *peers),
        micros=5,
    )

    block_at = jnp.minimum(plane_at, head_blocks - 1) * BLK
    bias_heads = lax.dynamic_slice_in_dim(b_qkv, block_at, BLK, 1).reshape(1, 3 * BLK)
    head_message = shape((PLANE * owned if direct else model, 4 * BLK), BF16)
    att, gp, wa, gb, *head_messages = kernel_call(
        partial(attention_kernel, direct),
        [
            shape((rows_all, BLK), BF16),
            shape((rows_all, 3 * BLK), BF16),
            shape((model, 4 * BLK), BF16),
            shape((1, 3 * BLK), F32),
        ]
        + [head_message] * max(direct, 1),
        1,
        (place_s, lengths, x1, g, bias_heads, *rotary_tables(slots), *head_pieces),
        scratch=[pltpu.VMEM((model, 4 * BLK), BF16)],
        micros=8,
    )

    bias_up = lax.dynamic_slice_in_dim(b_up, plane_at * width, width, 0).reshape(1, width)
    feed_message = shape((PLANE * owned + NOTES if direct else model, 2 * width), BF16)
    keep, send, notes, *feed_messages = kernel_call(
        partial(feed_kernel, direct),
        [
            shape((2, PLANE, own_rows, model), BF16),
            shape((2, PLANE, own_rows, model), BF16),
            shape((NOTES, model), F32),
        ]
        + [feed_message] * max(direct, 1),
        2,
        (place_s, half_s, params, x2, xh, g, wa, att, gp, bias_up, gb, bo, *feed_pieces),
        scratch=[
            pltpu.VMEM((model, 2 * width), BF16),
            pltpu.VMEM((model, 2 * width), BF16),
            pltpu.VMEM((rows_all, width), BF16),
            pltpu.VMEM((rows_all, width), BF16),
            pltpu.VMEM((2, slots, model), F32),
        ],
        micros=10.5,
    )

    summed = (keep.astype(F32) + to_peer(send).astype(F32)).astype(BF16)
    outgoing = [summed[:, k] for k in range(PLANE)]

    if direct:
        head_mid = to_pass(head_messages[2], back=True)
        head_near = to_level(head_messages[1], 1)
        feed_messages, head_mid = lax.optimization_barrier((feed_messages, head_mid))
        relayed = head_messages[3].astype(F32) + jnp.where(inner, head_mid.astype(F32), 0.0)
        head_far = to_level(relayed.astype(BF16), 3)
        feed_mid = to_pass(feed_messages[2], back=True)
        feed_near = to_level(feed_messages[1], 1)
        (feed_mid, head_mid), outgoing = lax.optimization_barrier(((feed_mid, head_mid), outgoing))
        rows = PLANE * owned
        relayed = feed_messages[3].astype(F32) + jnp.where(inner, feed_mid.astype(F32), 0.0)
        relayed = [relayed[:rows].astype(BF16), feed_messages[3][rows:], feed_mid[rows:]]
        feed_far = to_level(jnp.concatenate(relayed, axis=0), 3)
        columns = 4 * BLK + 2 * width
        backs = kernel_call(
            combine_kernel,
            [shape((owned + NOTES, columns), F32)] + [shape((owned + NOTES, columns), BF16)] * (PLANE - 1),
            1,
            (
                inner.astype(jnp.int32).reshape(1),
                *(head_messages[0], head_near, head_mid, head_far),
                *(feed_messages[0], feed_near, feed_mid, feed_far),
            ),
        )
    else:
        sums = jnp.concatenate([head_messages[0], feed_messages[0]], axis=1)
        sums = lax.psum_scatter(sums, "dp", scatter_dimension=0, tiled=True, axis_index_groups=level_groups)
        notes = lax.all_gather(notes.astype(BF16), "dp", axis=0, axis_index_groups=level_groups)
        notes = jnp.sum(notes.astype(F32), axis=0).astype(BF16)
        notes = jnp.concatenate([jnp.zeros((NOTES, 4 * BLK), BF16), notes], axis=1)
        sums = sums.reshape(PLANE, owned, 4 * BLK + 2 * width)
        backs = [
            jnp.concatenate([lax.dynamic_index_in_dim(sums, plane_at ^ k, 0, keepdims=False), notes], axis=0)
            for k in range(PLANE)
        ]
    parts = [outgoing[0]] + [to_plane(outgoing[k], k) for k in range(1, PLANE)]
    backs, parts = lax.optimization_barrier((backs, parts))
    backs = [backs[0]] + [to_plane(backs[k], k) for k in range(1, PLANE)]
    grad_up, grad_down, grad_qkv, grad_out_w, grad_b_up, grad_b_qkv, common = kernel_call(
        owner_kernel,
        [
            shape((owned, PLANE * width), F32),
            shape((owned, PLANE * width), F32),
            shape((3, owned, head_blocks * BLK), F32),
            shape((owned, head_blocks * BLK), F32),
            shape((1, PLANE * width), F32),
            shape((3, head_blocks * BLK), F32),
            shape((NOTES, model), F32),
        ],
        1,
        (place_s, *backs),
    )
    common = common + to_peer(common)

    branch, grad_norm = tree_sum([part.astype(F32) for part in parts])
    residual_f = residual.astype(F32)
    result = (residual_f + (branch + b_out + b_down)).astype(BF16)
    centre = jnp.mean(residual_f, axis=-1, keepdims=True)
    off = residual_f - centre
    scale = lax.rsqrt(jnp.mean(off * off, axis=-1, keepdims=True) + eps)
    xh_own = off * scale
    grad_residual = g_own.astype(F32) + scale * (
        grad_norm
        - jnp.mean(grad_norm, axis=-1, keepdims=True)
        - xh_own * jnp.mean(grad_norm * xh_own, axis=-1, keepdims=True)
    )
    return (
        result,
        grad_residual,
        common[2],
        common[3],
        common[4],
        common[5],
        grad_qkv,
        grad_b_qkv,
        grad_out_w.T,
        common[1],
        grad_up,
        grad_b_up[0],
        grad_down.T,
        common[1],
    )


def solution(mesh):
    return jax.shard_map(
        per_device,
        mesh=mesh,
        in_specs=(
            P(("dp", "tensor"), None),
            P(("dp", "tensor"), None),
            P("dp", None),
            P(),
            P(),
            P(),
            P(),
            P(None, "dp", "tensor"),
            P(None, "tensor"),
            P("tensor", "dp"),
            P(),
            P("dp", "tensor"),
            P("tensor"),
            P("tensor", "dp"),
            P(),
        ),
        out_specs=(
            P(("dp", "tensor"), None),
            P(("dp", "tensor"), None),
            P(),
            P(),
            P(),
            P(),
            P(None, "dp", "tensor"),
            P(None, "tensor"),
            P("tensor", "dp"),
            P(),
            P("dp", "tensor"),
            P("tensor"),
            P("tensor", "dp"),
            P(),
        ),
        check_vma=False,
    )
```

```python
import math
from functools import partial

import jax
import jax.numpy as jnp
import numpy as np
from jax import lax
from jax.experimental import pallas as pl
from jax.experimental.pallas import tpu as pltpu
from jax.sharding import PartitionSpec as P

HD = 64
ROT = 16
PLANE = 4
BLK = 2 * HD
NOTES = 16
eps = 1e-05
F32 = jnp.float32
BF16 = jnp.bfloat16


def dot(a, b):
    return jnp.dot(a, b, preferred_element_type=F32)


def dot_nt(a, b):
    return lax.dot_general(a, b, (((1,), (1,)), ((), ())), preferred_element_type=F32)


def dot_tn(a, b):
    return lax.dot_general(a, b, (((0,), (0,)), ((), ())), preferred_element_type=F32)


def place():
    index = lax.axis_index("dp")
    return index % PLANE, index // PLANE


def is_inner():
    level = place()[1]
    return (level == 1) | (level == 2)


def xor_sorted(parts, index):
    parts = list(parts)
    bit = 1
    while bit < len(parts):
        swap = (index & bit) != 0
        parts = [jnp.where(swap, parts[j ^ bit], parts[j]) for j in range(len(parts))]
        bit *= 2
    return parts


def tree_sum(parts):
    parts = list(parts)
    while len(parts) > 1:
        parts = [parts[j] + parts[j + 1] for j in range(0, len(parts), 2)]
    return parts[0]


def rotary_tables(rows):
    half = ROT // 2
    inverse = np.float32(10000.0) ** (-np.arange(half, dtype=np.float32) * np.float32(2.0 / ROT))
    angle = np.arange(rows, dtype=np.float32)[:, None] * inverse.astype(np.float32)[None, :]
    cos, sin = np.cos(angle), np.sin(angle)
    rest = np.ones((rows, HD - ROT), np.float32)
    none = np.zeros((rows, half), np.float32)
    keep = np.concatenate([cos, cos, rest], axis=1)
    low = np.concatenate([-sin, none, 0.0 * rest], axis=1)
    high = np.concatenate([none, sin, 0.0 * rest], axis=1)
    return tuple(
        np.concatenate([t] * (BLK // HD), axis=1).astype(np.float32) for t in (keep, low, high)
    )


def share_kernel(*refs):
    whole_refs, share_refs = refs[:4], refs[4 : 4 + PLANE]
    held_refs, arrived = refs[4 + PLANE : -1], refs[-1]
    copies = [
        pltpu.make_async_copy(whole, held, arrived.at[j])
        for j, (whole, held) in enumerate(zip(whole_refs, held_refs))
    ]
    for copy in copies:
        copy.start()
    for copy in copies:
        copy.wait()
    qkv_ref, out_ref, up_ref, down_ref = held_refs
    head_blocks = out_ref.shape[1] // BLK
    width = up_ref.shape[1] // PLANE
    for k in range(PLANE):
        other = place()[0] ^ k
        at = pl.ds(pl.multiple_of(jnp.minimum(other, head_blocks - 1) * BLK, BLK), BLK)
        for c in range(4):
            block = qkv_ref[c, :, at] if c < 3 else out_ref[:, at]
            block = jnp.where(other < head_blocks, block.astype(F32), 0.0)
            share_refs[k][:, c * BLK : (c + 1) * BLK] = block.astype(BF16)
        at = pl.ds(pl.multiple_of(other * width, BLK), width)
        share_refs[k][:, 4 * BLK : 4 * BLK + width] = up_ref[:, at]
        share_refs[k][:, 4 * BLK + width :] = down_ref[:, at]


def rows_at(m, k, owned):
    plane_at, level_at = place()
    return pl.ds(pl.multiple_of(((level_at ^ m) * PLANE + (plane_at ^ k)) * owned, owned), owned)


def rows_kernel(params_ref, own_ref, peer_ref, x1_ref, x2_ref, xh_ref, g_ref, g_own_ref, length_ref, bo_ref):
    half = lax.axis_index("tensor")
    own_rows = g_own_ref.shape[0]
    slots = 2 * own_rows
    params = params_ref[...]
    length_ref[...] = jnp.zeros_like(length_ref)
    for k in range(PLANE):
        start = k * (slots + NOTES)
        length = own_ref[start + slots : start + slots + NOTES, :].astype(F32)
        length = jnp.sum(length[0:1], axis=-1, keepdims=True)
        length_ref[k : k + 1, :] = jnp.broadcast_to(length, (1, length_ref.shape[1]))
        for which, ref in enumerate((own_ref, peer_ref)):
            part = half if which == 0 else 1 - half
            x = ref[start : start + own_rows, :].astype(F32)
            centre = jnp.mean(x, axis=-1, keepdims=True)
            off = x - centre
            spread = jnp.mean(off * off, axis=-1, keepdims=True)
            xh = off * lax.rsqrt(spread + eps)
            at = pl.ds(pl.multiple_of(k * slots + part * own_rows, own_rows), own_rows)
            x1_ref[at, :] = (xh * params[0:1] + params[1:2]).astype(BF16)
            x2_ref[at, :] = (xh * params[2:3] + params[3:4]).astype(BF16)
            xh_ref[at, :] = xh.astype(BF16)
            row = lax.broadcasted_iota(jnp.int32, (own_rows, 1), 0) + part * own_rows
            g = ref[start + own_rows : start + slots, :].astype(F32)
            g = jnp.where(row.astype(F32) < length, g, 0.0)
            g_ref[at, :] = g.astype(BF16)
            if k == 0 and which == 0:
                g_own_ref[...] = g.astype(BF16)
                bo_ref[...] = jnp.sum(g, axis=0, keepdims=True)


def layer_kernel(levels, *refs):
    length_ref, x1_ref, x2_ref, g_ref, bias_ref, bias_up_ref, keep_ref, low_ref, high_ref = refs[:9]
    pieces = refs[9 : 9 + max(2 * levels, 1)]
    att_ref, gp_ref, act_ref, gh_ref, w_ref, gb_ref = refs[9 + len(pieces) : 15 + len(pieces)]
    message_refs, gw_ref = refs[15 + len(pieces) : -1], refs[-1]
    if levels:
        owned = pieces[0].shape[0]
        for m in range(levels):
            w_ref[rows_at(m, 0, owned), :] = pieces[m][...]
            for k in range(1, PLANE):
                w_ref[rows_at(m, k, owned), :] = pieces[levels + m][(k - 1) * owned : k * owned, :]
    else:
        w_ref[...] = pieces[0][...]
        gw_ref = message_refs[0]
    heads, width = 4 * BLK, bias_up_ref.shape[1]
    slots = keep_ref.shape[0]
    keep, low, high = keep_ref[...], low_ref[...], high_ref[...]

    def turn(x, sign):
        return x * keep + sign * (
            pltpu.roll(x, BLK - ROT // 2, 1) * low + pltpu.roll(x, ROT // 2, 1) * high
        )

    lane = lax.broadcasted_iota(jnp.int32, (slots, BLK), 1)
    first = lane < HD
    q_row = lax.broadcasted_iota(jnp.int32, (2 * slots, slots), 0) & (slots - 1)
    k_row = lax.broadcasted_iota(jnp.int32, (2 * slots, slots), 1)

    def stacked(x):
        zero = jnp.zeros_like(x)
        return jnp.concatenate([jnp.where(first, x, zero), jnp.where(first, zero, x)], axis=0)

    def joined(x):
        return jnp.where(first, x[:slots], x[slots:])

    total = jnp.zeros((1, 3 * BLK), F32)
    for k in range(PLANE):
        at = pl.ds(k * slots, slots)
        proj = dot(x1_ref[at, :], w_ref[:, : 3 * BLK]) + bias_ref[...]
        query = stacked((turn(proj[:, :BLK], 1.0) * HD**-0.5).astype(BF16))
        key = turn(proj[:, BLK : 2 * BLK], 1.0).astype(BF16)
        value = proj[:, 2 * BLK :].astype(BF16)
        ga = stacked(dot(g_ref[at, :], w_ref[:, 3 * BLK : heads]).astype(BF16))
        logits = dot_nt(query, key)
        live = k_row.astype(F32) < length_ref[k : k + 1, 0:1]
        allowed = (k_row <= q_row) & (live | (k_row == q_row))
        logits = jnp.where(allowed, logits, -1000000000.0)
        weights = jnp.exp(logits - jnp.max(logits, axis=-1, keepdims=True))
        probs = weights / jnp.sum(weights, axis=-1, keepdims=True)
        rounded = probs.astype(BF16)
        att_ref[at, :] = joined(dot(rounded, value)).astype(BF16)
        grad_probs = dot_nt(ga, value)
        inner = jnp.sum(probs * grad_probs, axis=-1, keepdims=True)
        grad_logits = (probs * (grad_probs - inner)).astype(BF16)
        grad_query = joined(dot(grad_logits, key)) * HD**-0.5
        grad_key = dot_tn(grad_logits, query)
        grad_value = dot_tn(rounded, ga)
        gp = jnp.concatenate([turn(grad_query, -1.0), turn(grad_key, -1.0), grad_value], axis=1).astype(BF16)
        gp_ref[at, :] = gp
        total = total + jnp.sum(gp.astype(F32), axis=0, keepdims=True)
    gb_ref[:, width:] = total
    total = jnp.zeros((1, width), F32)
    for k in range(PLANE):
        at = pl.ds(k * slots, slots)
        hidden = dot(x2_ref[at, :], w_ref[:, heads : heads + width]) + bias_up_ref[...]
        grad_act = dot(g_ref[at, :], w_ref[:, heads + width :])
        part = 0.5 + 0.5 * lax.erf(hidden * (0.5**0.5))
        act_ref[at, :] = (hidden * part).astype(BF16)
        slope = part + hidden * jnp.exp(-0.5 * hidden * hidden) * (2.0 * math.pi) ** -0.5
        gh = (grad_act * slope).astype(BF16)
        gh_ref[at, :] = gh
        total = total + jnp.sum(gh.astype(F32), axis=0, keepdims=True)
    gb_ref[:, :width] = total
    gw_ref[:, : 3 * BLK] = dot_tn(x1_ref[...], gp_ref[...]).astype(BF16)
    gw_ref[:, 3 * BLK : heads] = dot_tn(g_ref[...], att_ref[...]).astype(BF16)
    gw_ref[:, heads : heads + width] = dot_tn(x2_ref[...], gh_ref[...]).astype(BF16)
    gw_ref[:, heads + width :] = dot_tn(g_ref[...], act_ref[...]).astype(BF16)
    if levels:
        for m in range(levels):
            for k in range(PLANE):
                message_refs[m][k * owned : (k + 1) * owned, :] = gw_ref[rows_at(m, k, owned), :]


def products_kernel(
    params_ref, xh_ref, w_ref, act_ref, gh_ref, att_ref, gp_ref, gb_ref, bo_ref, keep_ref, send_ref, stage_ref
):
    half = lax.axis_index("tensor")
    slots = stage_ref.shape[1]
    own_rows = slots // 2
    heads, width = 4 * BLK, act_ref.shape[1]
    params = params_ref[...]
    gain1, gain2 = params[0:1], params[2:3]
    sums = [jnp.zeros((1, xh_ref.shape[1]), F32) for _ in range(4)]
    for k in range(PLANE):
        at = pl.ds(k * slots, slots)
        stage_ref[0] = dot_nt(act_ref[at, :], w_ref[:, heads + width :]) + dot_nt(
            att_ref[at, :], w_ref[:, 3 * BLK : heads]
        )
        g1 = dot_nt(gp_ref[at, :], w_ref[:, : 3 * BLK])
        g2 = dot_nt(gh_ref[at, :], w_ref[:, heads : heads + width])
        stage_ref[1] = gain1 * g1 + gain2 * g2
        xh = xh_ref[at, :].astype(F32)
        for j, term in enumerate((g1 * xh, g1, g2 * xh, g2)):
            sums[j] = sums[j] + jnp.sum(term, axis=0, keepdims=True)
        mine = pl.ds(pl.multiple_of(half * own_rows, own_rows), own_rows)
        other = pl.ds(pl.multiple_of((1 - half) * own_rows, own_rows), own_rows)
        for j in range(2):
            to = pl.ds(k * slots + j * own_rows, own_rows)
            keep_ref[to, :] = stage_ref[j, mine, :].astype(BF16)
            send_ref[to, :] = stage_ref[j, other, :].astype(BF16)
    zero = jnp.zeros((NOTES - 6, xh_ref.shape[1]), F32)
    notes = jnp.concatenate([gb_ref[...], bo_ref[...]] + sums + [zero], axis=0).astype(BF16)
    keep_ref[PLANE * slots :, :] = notes
    send_ref[PLANE * slots :, :] = notes


def pair_kernel(levels, keep_ref, peer_ref, *refs):
    notes_ref, out_refs = refs[-PLANE - 1], refs[-PLANE:]
    slots = out_refs[0].shape[0]
    notes = keep_ref[PLANE * slots :, :].astype(F32)
    row = lax.broadcasted_iota(jnp.int32, notes.shape, 0)
    notes = notes + jnp.where(row == 0, 0.0, peer_ref[PLANE * slots :, :].astype(F32))
    notes = notes.astype(BF16)
    notes_ref[...] = notes
    for k, out_ref in enumerate(out_refs):
        at = pl.ds(k * slots, slots)
        out_ref[...] = (keep_ref[at, :].astype(F32) + peer_ref[at, :].astype(F32)).astype(BF16)
    if levels:
        passed_ref, near_ref, far_ref, to_near_ref, to_far_ref = refs[:5]
        rows, columns = near_ref.shape
        passed = jnp.where(is_inner(), passed_ref[...].astype(F32), 0.0)
        to_near_ref[:rows, :] = near_ref[...]
        to_far_ref[:rows, :] = (far_ref[...].astype(F32) + passed).astype(BF16)
        notes = jnp.concatenate([jnp.zeros((NOTES, columns - notes.shape[1]), BF16), notes], axis=1)
        to_near_ref[rows:, :] = notes
        to_far_ref[rows:, :] = notes


def rows_out_kernel(residual_ref, g_ref, b_out_ref, b_down_ref, *refs):
    part_refs, (result_ref, grad_ref) = refs[:PLANE], refs[PLANE:]
    own_rows = residual_ref.shape[0]
    branch = tree_sum([ref[:own_rows, :].astype(F32) for ref in part_refs])
    x = residual_ref[...].astype(F32)
    result_ref[...] = (x + (branch + b_out_ref[...] + b_down_ref[...])).astype(BF16)
    off = x - jnp.mean(x, axis=-1, keepdims=True)
    scale = lax.rsqrt(jnp.mean(off * off, axis=-1, keepdims=True) + eps)
    xh = off * scale
    grad = tree_sum([ref[own_rows:, :].astype(F32) for ref in part_refs])
    grad = grad - jnp.mean(grad, axis=-1, keepdims=True) - xh * jnp.mean(grad * xh, axis=-1, keepdims=True)
    grad_ref[...] = g_ref[...].astype(F32) + scale * grad


def combine_kernel(own_ref, near_ref, passed_ref, far_ref, notes_ref, notes_middle_ref, *out_refs):
    rows = own_ref.shape[0]
    owned = rows // PLANE
    columns, model = own_ref.shape[1], notes_ref.shape[1]
    passed_here = jnp.logical_not(is_inner())
    own, middle = notes_ref[...].astype(F32), notes_middle_ref[...].astype(F32)
    near, far = [ref[rows:, columns - model :].astype(F32) for ref in (near_ref, far_ref)]
    notes = ((own + near) + (middle + far)).astype(BF16)
    for k, out_ref in enumerate(out_refs):
        at = pl.ds(k * owned, owned)
        total = own_ref[at, :].astype(F32) + near_ref[at, :].astype(F32) + far_ref[at, :].astype(F32)
        total = total + jnp.where(passed_here, passed_ref[at, :].astype(F32), 0.0)
        out_ref[:owned, :] = total.astype(out_ref.dtype)
        out_ref[owned:, : columns - model] = jnp.zeros((NOTES, columns - model), out_ref.dtype)
        out_ref[owned:, columns - model :] = notes.astype(out_ref.dtype)


def owner_kernel(*refs):
    part_refs = refs[:PLANE]
    up_ref, down_ref, qkv_ref, out_ref, b_up_ref, b_qkv_ref, common_ref = refs[PLANE:]
    owned = up_ref.shape[0]
    width = up_ref.shape[1] // PLANE
    head_blocks = out_ref.shape[1] // BLK
    start = 4 * BLK
    for k, part_ref in enumerate(part_refs):
        other = place()[0] ^ k
        at = pl.ds(pl.multiple_of(other * width, BLK), width)
        up_ref[:, at] = part_ref[:owned, start : start + width].astype(F32)
        down_ref[:, at] = part_ref[:owned, start + width :].astype(F32)
        notes = part_ref[owned:, start:].astype(F32)
        b_up_ref[:, at] = notes[0:1, :width]

        @pl.when(other < head_blocks)
        def _():
            at = pl.ds(pl.multiple_of(other * BLK, BLK), BLK)
            for c in range(3):
                qkv_ref[c, :, at] = part_ref[:owned, c * BLK : (c + 1) * BLK].astype(F32)
                b_qkv_ref[c : c + 1, at] = notes[0:1, width + c * BLK : width + (c + 1) * BLK]
            out_ref[:, at] = part_ref[:owned, 3 * BLK : 4 * BLK].astype(F32)

    common_ref[...] = tree_sum([ref[owned:, start:].astype(F32) for ref in part_refs])


def kernel_call(body, out_shapes, operands, scratch=(), micros=1.0, space=pltpu.VMEM, limit=20):
    vmem = pl.BlockSpec(memory_space=pltpu.VMEM)
    taken = pl.BlockSpec(memory_space=space)
    return pl.pallas_call(
        body,
        out_shape=out_shapes,
        in_specs=[taken] * len(operands),
        out_specs=[vmem] * len(out_shapes),
        scratch_shapes=list(scratch),
        compiler_params=pltpu.CompilerParams(vmem_limit_bytes=limit * 2**20),
        cost_estimate=pl.CostEstimate(flops=int(micros * 1e9), bytes_accessed=1, transcendentals=0),
    )(*operands)


def per_device(
    residual,
    cotangent,
    seq_lengths,
    gain_attn,
    shift_attn,
    gain_mlp,
    shift_mlp,
    w_qkv,
    b_qkv,
    w_out,
    b_out,
    w_up,
    b_up,
    w_down,
    b_down,
):
    places = lax.axis_size("dp")
    levels = places // PLANE
    plane_at = place()[0]
    own_rows, model = residual.shape
    slots = 2 * own_rows
    rows_all = PLANE * slots
    owned = w_up.shape[0]
    width = w_up.shape[1] // PLANE
    head_blocks = w_out.shape[0] // BLK
    columns = 4 * BLK + 2 * width
    direct = levels if levels == 4 and owned % 16 == 0 else 0
    level_groups = [[lev * PLANE + j for lev in range(levels)] for j in range(PLANE)]
    shape = jax.ShapeDtypeStruct

    def to_plane(x, k):
        return lax.ppermute(x, "dp", [(j, j ^ k) for j in range(places)])

    def to_level(x, m):
        return lax.ppermute(x, "dp", [(j, j ^ (m * PLANE)) for j in range(places)])

    def to_peer(x):
        return lax.ppermute(x, "tensor", [(0, 1), (1, 0)])

    passing = [(0, 2), (3, 1), (1, 0), (2, 3)]

    def to_pass(x, back=False):
        pairs = [(b, a) if back else (a, b) for a, b in passing]
        return lax.ppermute(x, "dp", [(a * PLANE + j, b * PLANE + j) for a, b in pairs for j in range(PLANE)])

    held = (w_qkv, w_out.T, w_up, w_down.T)
    shares = kernel_call(
        share_kernel,
        [shape((owned, columns), BF16)] * PLANE,
        held,
        scratch=[pltpu.VMEM(a.shape, a.dtype) for a in held] + [pltpu.SemaphoreType.DMA((4,))],
        space=pl.ANY,
        limit=63,
    )
    received = [to_plane(shares[k], k) for k in range(1, PLANE)]
    residual_m, cotangent_m, lengths_m, _ = lax.optimization_barrier((residual, cotangent, seq_lengths, shares))
    notes = jnp.pad(lengths_m.astype(BF16), ((0, NOTES - 1), (0, model - seq_lengths.shape[1])))
    message = jnp.concatenate([residual_m, cotangent_m, notes], axis=0)
    if direct:
        own = shares[0]
        own_near, own_far = to_level(own, 1), to_level(own, 3)
        received, own, own_near, own_far, message = lax.optimization_barrier(
            (received, own, own_near, own_far, message)
        )
        others = jnp.concatenate(received, axis=0)
        near, far = to_level(others, 1), to_level(others, 3)
        own_mid = to_pass(jnp.where(is_inner(), own_far, own))
    messages = [message] + [to_plane(message, k) for k in range(1, PLANE)]
    if direct:
        messages, own_mid, near, far = lax.optimization_barrier((messages, own_mid, near, far))
        mid = to_pass(jnp.where(is_inner(), far, others))
        pieces = [own, own_near, own_mid, own_far, others, near, mid, far]
    else:
        every = jnp.concatenate(xor_sorted([shares[0]] + received, plane_at), axis=0)
        pieces = [lax.all_gather(every, "dp", axis=0, tiled=True, axis_index_groups=level_groups)]
    rows = jnp.concatenate(messages, axis=0)
    params = jnp.stack([gain_attn, shift_attn, gain_mlp, shift_mlp] + [jnp.zeros_like(gain_attn)] * 4)
    x1, x2, xh, g, g_own, lengths, bo = kernel_call(
        rows_kernel,
        [shape((rows_all, model), BF16)] * 4
        + [shape((own_rows, model), BF16), shape((8, 128), F32), shape((1, model), F32)],
        (params, rows, to_peer(rows)),
        micros=4,
    )

    block_at = jnp.minimum(plane_at, head_blocks - 1) * BLK
    bias_heads = lax.dynamic_slice_in_dim(b_qkv, block_at, BLK, 1).reshape(1, 3 * BLK)
    bias_up = lax.dynamic_slice_in_dim(b_up, plane_at * width, width, 0).reshape(1, width)
    att, gp, act, gh, w, gb, *messages = kernel_call(
        partial(layer_kernel, direct),
        [
            shape((rows_all, BLK), BF16),
            shape((rows_all, 3 * BLK), BF16),
            shape((rows_all, width), BF16),
            shape((rows_all, width), BF16),
            shape((model, columns), BF16),
            shape((1, width + 3 * BLK), F32),
        ]
        + [shape((PLANE * owned if direct else model, columns), BF16)] * max(direct, 1),
        (lengths, x1, x2, g, bias_heads, bias_up, *rotary_tables(slots), *pieces),
        scratch=[pltpu.VMEM((model, columns), BF16)],
        micros=12,
        limit=30,
    )
    if direct:
        passed = to_pass(messages[2], back=True)
    keep, send = kernel_call(
        products_kernel,
        [shape((rows_all + NOTES, model), BF16)] * 2,
        (params, xh, w, act, gh, att, gp, gb, bo),
        scratch=[pltpu.VMEM((2, slots, model), F32)],
        micros=4,
    )
    from_peer = to_peer(send)
    extra, extra_shapes = (), []
    if direct:
        passed, from_peer = lax.optimization_barrier((passed, from_peer))
        extra = (passed, messages[1], messages[3])
        extra_shapes = [shape((PLANE * owned + NOTES, columns), BF16)] * 2
    laid = kernel_call(
        partial(pair_kernel, direct),
        extra_shapes + [shape((NOTES, model), BF16)] + [shape((slots, model), BF16)] * PLANE,
        (keep, from_peer, *extra),
        micros=2,
    )

    notes, outgoing = laid[-PLANE - 1], laid[-PLANE:]

    parts = [outgoing[0]] + [to_plane(outgoing[k], k) for k in range(1, PLANE)]
    if direct:
        near, far = to_level(laid[0], 1), to_level(laid[1], 3)
        notes_after, parts[1] = lax.optimization_barrier((notes, parts[1]))
        notes_mid = to_level(notes_after, 2)
        parts, near, far, notes_mid = lax.optimization_barrier((parts, near, far, notes_mid))
        backs = kernel_call(
            combine_kernel,
            [shape((owned + NOTES, columns), F32)] + [shape((owned + NOTES, columns), BF16)] * (PLANE - 1),
            (messages[0], near, passed, far, notes, notes_mid),
        )
    else:
        sums = lax.psum_scatter(
            messages[0], "dp", scatter_dimension=0, tiled=True, axis_index_groups=level_groups
        ).reshape(PLANE, owned, columns)
        notes = lax.all_gather(notes, "dp", axis=0, axis_index_groups=level_groups)
        notes = jnp.sum(notes.astype(F32), axis=0).astype(BF16)
        notes = jnp.concatenate([jnp.zeros((NOTES, columns - model), BF16), notes], axis=1)
        backs = [
            jnp.concatenate([lax.dynamic_index_in_dim(sums, plane_at ^ k, 0, keepdims=False), notes], axis=0)
            for k in range(PLANE)
        ]
    backs = [backs[0]] + [to_plane(backs[k], k) for k in range(1, PLANE)]
    result, grad_residual = kernel_call(
        rows_out_kernel,
        [shape((own_rows, model), BF16), shape((own_rows, model), F32)],
        (residual, g_own, b_out.reshape(1, model), b_down.reshape(1, model), *parts),
    )
    grad_up, grad_down, grad_qkv, grad_out_w, grad_b_up, grad_b_qkv, common = kernel_call(
        owner_kernel,
        [
            shape((owned, PLANE * width), F32),
            shape((owned, PLANE * width), F32),
            shape((3, owned, head_blocks * BLK), F32),
            shape((owned, head_blocks * BLK), F32),
            shape((1, PLANE * width), F32),
            shape((3, head_blocks * BLK), F32),
            shape((NOTES, model), F32),
        ],
        backs,
    )
    return (
        result,
        grad_residual,
        common[2],
        common[3],
        common[4],
        common[5],
        grad_qkv,
        grad_b_qkv,
        grad_out_w.T,
        common[1],
        grad_up,
        grad_b_up[0],
        grad_down.T,
        common[1],
    )


def solution(mesh):
    return jax.shard_map(
        per_device,
        mesh=mesh,
        in_specs=(
            P(("dp", "tensor"), None),
            P(("dp", "tensor"), None),
            P("dp", None),
            P(),
            P(),
            P(),
            P(),
            P(None, "dp", "tensor"),
            P(None, "tensor"),
            P("tensor", "dp"),
            P(),
            P("dp", "tensor"),
            P("tensor"),
            P("tensor", "dp"),
            P(),
        ),
        out_specs=(
            P(("dp", "tensor"), None),
            P(("dp", "tensor"), None),
            P(),
            P(),
            P(),
            P(),
            P(None, "dp", "tensor"),
            P(None, "tensor"),
            P("tensor", "dp"),
            P(),
            P("dp", "tensor"),
            P("tensor"),
            P("tensor", "dp"),
            P(),
        ),
        check_vma=False,
    )
```

```python
import math
from functools import partial

import jax
import jax.numpy as jnp
import numpy as np
from jax import lax
from jax.experimental import pallas as pl
from jax.experimental.pallas import tpu as pltpu
from jax.sharding import PartitionSpec as P

HD = 64
ROT = 16
PLANE = 4
BLK = 2 * HD
NOTES = 16
eps = 1e-05
F32 = jnp.float32
BF16 = jnp.bfloat16


def dot(a, b):
    return jnp.dot(a, b, preferred_element_type=F32)


def dot_nt(a, b):
    return lax.dot_general(a, b, (((1,), (1,)), ((), ())), preferred_element_type=F32)


def dot_tn(a, b):
    return lax.dot_general(a, b, (((0,), (0,)), ((), ())), preferred_element_type=F32)


def place():
    index = lax.axis_index("dp")
    return index % PLANE, index // PLANE


def is_inner():
    level = place()[1]
    return (level == 1) | (level == 2)


def xor_sorted(parts, index):
    parts = list(parts)
    bit = 1
    while bit < len(parts):
        swap = (index & bit) != 0
        parts = [jnp.where(swap, parts[j ^ bit], parts[j]) for j in range(len(parts))]
        bit *= 2
    return parts


def tree_sum(parts):
    parts = list(parts)
    while len(parts) > 1:
        parts = [parts[j] + parts[j + 1] for j in range(0, len(parts), 2)]
    return parts[0]


def rotary_tables(rows):
    half = ROT // 2
    inverse = np.float32(10000.0) ** (-np.arange(half, dtype=np.float32) * np.float32(2.0 / ROT))
    angle = np.arange(rows, dtype=np.float32)[:, None] * inverse.astype(np.float32)[None, :]
    cos, sin = np.cos(angle), np.sin(angle)
    rest = np.ones((rows, HD - ROT), np.float32)
    none = np.zeros((rows, half), np.float32)
    keep = np.concatenate([cos, cos, rest], axis=1)
    low = np.concatenate([-sin, none, 0.0 * rest], axis=1)
    high = np.concatenate([none, sin, 0.0 * rest], axis=1)
    return tuple(
        np.concatenate([t] * (BLK // HD), axis=1).astype(np.float32) for t in (keep, low, high)
    )


def share_kernel(*refs):
    whole_refs, share_refs = refs[:4], refs[4 : 4 + PLANE]
    held_refs, arrived = refs[4 + PLANE : -1], refs[-1]
    copies = [
        pltpu.make_async_copy(whole, held, arrived.at[j])
        for j, (whole, held) in enumerate(zip(whole_refs, held_refs))
    ]
    for copy in copies:
        copy.start()
    for copy in copies:
        copy.wait()
    qkv_ref, out_ref, up_ref, down_ref = held_refs
    head_blocks = out_ref.shape[1] // BLK
    width = up_ref.shape[1] // PLANE
    for k in range(PLANE):
        other = place()[0] ^ k
        heads, out = 3 * BLK, 3 * BLK + width
        at = pl.ds(pl.multiple_of(jnp.minimum(other, head_blocks - 1) * BLK, BLK), BLK)
        for c in range(4):
            block = qkv_ref[c, :, at] if c < 3 else out_ref[:, at]
            block = jnp.where(other < head_blocks, block.astype(F32), 0.0)
            start = c * BLK if c < 3 else out
            share_refs[k][:, start : start + BLK] = block.astype(BF16)
        at = pl.ds(pl.multiple_of(other * width, BLK), width)
        share_refs[k][:, heads:out] = up_ref[:, at]
        share_refs[k][:, out + BLK :] = down_ref[:, at]


def rows_at(m, k, owned):
    plane_at, level_at = place()
    return pl.ds(pl.multiple_of(((level_at ^ m) * PLANE + (plane_at ^ k)) * owned, owned), owned)


def rows_kernel(params_ref, own_ref, peer_ref, x1_ref, x2_ref, xh_ref, g_ref, g_own_ref, length_ref, bo_ref):
    half = lax.axis_index("tensor")
    own_rows = g_own_ref.shape[0]
    slots = 2 * own_rows
    params = params_ref[...]
    length_ref[...] = jnp.zeros_like(length_ref)
    for k in range(PLANE):
        start = k * (slots + NOTES)
        length = own_ref[start + slots : start + slots + NOTES, :].astype(F32)
        length = jnp.sum(length[0:1], axis=-1, keepdims=True)
        length_ref[k : k + 1, :] = jnp.broadcast_to(length, (1, length_ref.shape[1]))
        for which, ref in enumerate((own_ref, peer_ref)):
            part = half if which == 0 else 1 - half
            x = ref[start : start + own_rows, :].astype(F32)
            centre = jnp.mean(x, axis=-1, keepdims=True)
            off = x - centre
            spread = jnp.mean(off * off, axis=-1, keepdims=True)
            xh = off * lax.rsqrt(spread + eps)
            at = pl.ds(pl.multiple_of(k * slots + part * own_rows, own_rows), own_rows)
            x1_ref[at, :] = (xh * params[0:1] + params[1:2]).astype(BF16)
            x2_ref[at, :] = (xh * params[2:3] + params[3:4]).astype(BF16)
            xh_ref[at, :] = xh.astype(BF16)
            row = lax.broadcasted_iota(jnp.int32, (own_rows, 1), 0) + part * own_rows
            g = ref[start + own_rows : start + slots, :].astype(F32)
            g = jnp.where(row.astype(F32) < length, g, 0.0)
            g_ref[at, :] = g.astype(BF16)
            if k == 0 and which == 0:
                g_own_ref[...] = g.astype(BF16)
                bo_ref[...] = jnp.sum(g, axis=0, keepdims=True)


def layer_kernel(levels, *refs):
    length_ref, x1_ref, x2_ref, g_ref, bias_ref, bias_up_ref, keep_ref, low_ref, high_ref = refs[:9]
    pieces = refs[9 : 9 + max(2 * levels, 1)]
    za_ref, gp_ref, gh_ref, w_ref, gb_ref = refs[9 + len(pieces) : 14 + len(pieces)]
    message_refs, gw_ref = refs[14 + len(pieces) : -1], refs[-1]
    if levels:
        owned = pieces[0].shape[0]
        for m in range(levels):
            w_ref[rows_at(m, 0, owned), :] = pieces[m][...]
            for k in range(1, PLANE):
                w_ref[rows_at(m, k, owned), :] = pieces[levels + m][(k - 1) * owned : k * owned, :]
    else:
        w_ref[...] = pieces[0][...]
        gw_ref = message_refs[0]
    width = bias_up_ref.shape[1]
    heads, out = 3 * BLK, 3 * BLK + width
    slots = keep_ref.shape[0]
    keep, low, high = keep_ref[...], low_ref[...], high_ref[...]

    def turn(x, sign):
        return x * keep + sign * (
            pltpu.roll(x, BLK - ROT // 2, 1) * low + pltpu.roll(x, ROT // 2, 1) * high
        )

    lane = lax.broadcasted_iota(jnp.int32, (slots, BLK), 1)
    first = lane < HD
    q_row = lax.broadcasted_iota(jnp.int32, (2 * slots, slots), 0) & (slots - 1)
    k_row = lax.broadcasted_iota(jnp.int32, (2 * slots, slots), 1)

    def stacked(x):
        zero = jnp.zeros_like(x)
        return jnp.concatenate([jnp.where(first, x, zero), jnp.where(first, zero, x)], axis=0)

    def joined(x):
        return jnp.where(first, x[:slots], x[slots:])

    total = jnp.zeros((1, 3 * BLK), F32)
    total_up = jnp.zeros((1, width), F32)
    for k in range(PLANE):
        at = pl.ds(k * slots, slots)
        proj = dot(x1_ref[at, :], w_ref[:, :heads]) + bias_ref[...]
        hidden = dot(x2_ref[at, :], w_ref[:, heads:out]) + bias_up_ref[...]
        back = dot(g_ref[at, :], w_ref[:, out:])
        query = stacked((turn(proj[:, :BLK], 1.0) * HD**-0.5).astype(BF16))
        key = turn(proj[:, BLK : 2 * BLK], 1.0).astype(BF16)
        value = proj[:, 2 * BLK :].astype(BF16)
        ga = stacked(back[:, :BLK].astype(BF16))
        logits = dot_nt(query, key)
        live = k_row.astype(F32) < length_ref[k : k + 1, 0:1]
        allowed = (k_row <= q_row) & (live | (k_row == q_row))
        logits = jnp.where(allowed, logits, -1000000000.0)
        weights = jnp.exp(logits - jnp.max(logits, axis=-1, keepdims=True))
        probs = weights / jnp.sum(weights, axis=-1, keepdims=True)
        rounded = probs.astype(BF16)
        za_ref[at, :BLK] = joined(dot(rounded, value)).astype(BF16)
        grad_probs = dot_nt(ga, value)
        inner = jnp.sum(probs * grad_probs, axis=-1, keepdims=True)
        grad_logits = (probs * (grad_probs - inner)).astype(BF16)
        grad_query = joined(dot(grad_logits, key)) * HD**-0.5
        grad_key = dot_tn(grad_logits, query)
        grad_value = dot_tn(rounded, ga)
        gp = jnp.concatenate([turn(grad_query, -1.0), turn(grad_key, -1.0), grad_value], axis=1).astype(BF16)
        gp_ref[at, :] = gp
        total = total + jnp.sum(gp.astype(F32), axis=0, keepdims=True)
        part = 0.5 + 0.5 * lax.erf(hidden * (0.5**0.5))
        za_ref[at, BLK:] = (hidden * part).astype(BF16)
        slope = part + hidden * jnp.exp(-0.5 * hidden * hidden) * (2.0 * math.pi) ** -0.5
        gh = (back[:, BLK:] * slope).astype(BF16)
        gh_ref[at, :] = gh
        total_up = total_up + jnp.sum(gh.astype(F32), axis=0, keepdims=True)
    gb_ref[:, :width] = total_up
    gb_ref[:, width:] = total
    gw_ref[:, :heads] = dot_tn(x1_ref[...], gp_ref[...]).astype(BF16)
    gw_ref[:, heads:out] = dot_tn(x2_ref[...], gh_ref[...]).astype(BF16)
    gw_ref[:, out:] = dot_tn(g_ref[...], za_ref[...]).astype(BF16)
    if levels:
        for m in range(levels):
            for k in range(PLANE):
                message_refs[m][k * owned : (k + 1) * owned, :] = gw_ref[rows_at(m, k, owned), :]


def products_kernel(
    params_ref, xh_ref, w_ref, za_ref, gp_ref, gh_ref, gb_ref, bo_ref, keep_ref, send_ref, stage_ref
):
    half = lax.axis_index("tensor")
    slots = stage_ref.shape[1]
    own_rows = slots // 2
    heads, out = 3 * BLK, 3 * BLK + gh_ref.shape[1]
    params = params_ref[...]
    gain1, gain2 = params[0:1], params[2:3]
    sums = [jnp.zeros((1, xh_ref.shape[1]), F32) for _ in range(4)]
    for k in range(PLANE):
        at = pl.ds(k * slots, slots)
        stage_ref[0] = dot_nt(za_ref[at, :], w_ref[:, out:])
        g1 = dot_nt(gp_ref[at, :], w_ref[:, :heads])
        g2 = dot_nt(gh_ref[at, :], w_ref[:, heads:out])
        stage_ref[1] = gain1 * g1 + gain2 * g2
        xh = xh_ref[at, :].astype(F32)
        for j, term in enumerate((g1 * xh, g1, g2 * xh, g2)):
            sums[j] = sums[j] + jnp.sum(term, axis=0, keepdims=True)
        mine = pl.ds(pl.multiple_of(half * own_rows, own_rows), own_rows)
        other = pl.ds(pl.multiple_of((1 - half) * own_rows, own_rows), own_rows)
        for j in range(2):
            to = pl.ds(k * slots + j * own_rows, own_rows)
            keep_ref[to, :] = stage_ref[j, mine, :].astype(BF16)
            send_ref[to, :] = stage_ref[j, other, :].astype(BF16)
    zero = jnp.zeros((NOTES - 6, xh_ref.shape[1]), F32)
    notes = jnp.concatenate([gb_ref[...], bo_ref[...]] + sums + [zero], axis=0).astype(BF16)
    keep_ref[PLANE * slots :, :] = notes
    send_ref[PLANE * slots :, :] = notes


def join_kernel(*refs):
    owned = refs[0].shape[0]
    for k, ref in enumerate(refs[:-1]):
        refs[-1][k * owned : (k + 1) * owned, :] = ref[...]


def choose_kernel(own_ref, far_ref, out_ref):
    out_ref[...] = jnp.where(is_inner(), far_ref[...].astype(F32), own_ref[...].astype(F32)).astype(BF16)


def relay_kernel(far_ref, passed_ref, out_ref):
    passed = jnp.where(is_inner(), passed_ref[...].astype(F32), 0.0)
    out_ref[...] = (far_ref[...].astype(F32) + passed).astype(BF16)


def pair_kernel(levels, keep_ref, peer_ref, *refs):
    notes_ref, out_refs = refs[-PLANE - 1], refs[-PLANE:]
    slots = out_refs[0].shape[0]
    notes = keep_ref[PLANE * slots :, :].astype(F32)
    row = lax.broadcasted_iota(jnp.int32, notes.shape, 0)
    notes = notes + jnp.where(row == 0, 0.0, peer_ref[PLANE * slots :, :].astype(F32))
    notes = notes.astype(BF16)
    notes_ref[...] = notes
    for k, out_ref in enumerate(out_refs):
        at = pl.ds(k * slots, slots)
        out_ref[...] = (keep_ref[at, :].astype(F32) + peer_ref[at, :].astype(F32)).astype(BF16)
    if levels:
        near_ref, far_ref, to_near_ref, to_far_ref = refs[:4]
        rows, columns = near_ref.shape
        to_near_ref[:rows, :] = near_ref[...]
        to_far_ref[:rows, :] = far_ref[...]
        notes = jnp.concatenate([jnp.zeros((NOTES, columns - notes.shape[1]), BF16), notes], axis=1)
        to_near_ref[rows:, :] = notes
        to_far_ref[rows:, :] = notes


def rows_out_kernel(residual_ref, g_ref, b_out_ref, b_down_ref, *refs):
    part_refs, (result_ref, grad_ref) = refs[:PLANE], refs[PLANE:]
    own_rows = residual_ref.shape[0]
    branch = tree_sum([ref[:own_rows, :].astype(F32) for ref in part_refs])
    x = residual_ref[...].astype(F32)
    result_ref[...] = (x + (branch + b_out_ref[...] + b_down_ref[...])).astype(BF16)
    off = x - jnp.mean(x, axis=-1, keepdims=True)
    scale = lax.rsqrt(jnp.mean(off * off, axis=-1, keepdims=True) + eps)
    xh = off * scale
    grad = tree_sum([ref[own_rows:, :].astype(F32) for ref in part_refs])
    grad = grad - jnp.mean(grad, axis=-1, keepdims=True) - xh * jnp.mean(grad * xh, axis=-1, keepdims=True)
    grad_ref[...] = g_ref[...].astype(F32) + scale * grad


def combine_kernel(own_ref, near_ref, passed_ref, far_ref, notes_ref, notes_middle_ref, *out_refs):
    rows = own_ref.shape[0]
    owned = rows // PLANE
    columns, model = own_ref.shape[1], notes_ref.shape[1]
    passed_here = jnp.logical_not(is_inner())
    own, middle = notes_ref[...].astype(F32), notes_middle_ref[...].astype(F32)
    near, far = [ref[rows:, columns - model :].astype(F32) for ref in (near_ref, far_ref)]
    notes = ((own + near) + (middle + far)).astype(BF16)
    for k, out_ref in enumerate(out_refs):
        at = pl.ds(k * owned, owned)
        total = own_ref[at, :].astype(F32) + near_ref[at, :].astype(F32) + far_ref[at, :].astype(F32)
        total = total + jnp.where(passed_here, passed_ref[at, :].astype(F32), 0.0)
        out_ref[:owned, :] = total.astype(out_ref.dtype)
        out_ref[owned:, : columns - model] = jnp.zeros((NOTES, columns - model), out_ref.dtype)
        out_ref[owned:, columns - model :] = notes.astype(out_ref.dtype)


def owner_kernel(*refs):
    part_refs = refs[:PLANE]
    up_ref, down_ref, qkv_ref, out_ref, b_up_ref, b_qkv_ref = refs[PLANE : PLANE + 6]
    common_refs = refs[PLANE + 6 :]
    owned = up_ref.shape[0]
    width = up_ref.shape[1] // PLANE
    head_blocks = out_ref.shape[1] // BLK
    heads, out = 3 * BLK, 3 * BLK + width
    all_notes = []
    for k, part_ref in enumerate(part_refs):
        other = place()[0] ^ k
        at = pl.ds(pl.multiple_of(other * width, BLK), width)
        up_ref[:, at] = part_ref[:owned, heads:out].astype(F32)
        down_ref[:, at] = part_ref[:owned, out + BLK :].astype(F32)
        notes = part_ref[owned:, part_ref.shape[1] - common_refs[0].shape[0] * BLK :].astype(F32)
        all_notes.append(notes)
        for j in range(width // BLK):
            b_up_ref[pl.ds(other * (width // BLK) + j, 1), :] = notes[0:1, j * BLK : (j + 1) * BLK]

        @pl.when(other < head_blocks)
        def _():
            at = pl.ds(pl.multiple_of(other * BLK, BLK), BLK)
            for c in range(3):
                qkv_ref[c, :, at] = part_ref[:owned, c * BLK : (c + 1) * BLK].astype(F32)
                b_qkv_ref[c : c + 1, at] = notes[0:1, width + c * BLK : width + (c + 1) * BLK]
            out_ref[:, at] = part_ref[:owned, out : out + BLK].astype(F32)

    common = tree_sum(all_notes)
    for row, common_ref in zip((1, 1, 2, 3, 4, 5), common_refs):
        for j in range(common_ref.shape[0]):
            common_ref[j : j + 1, :] = common[row : row + 1, j * BLK : (j + 1) * BLK]


def kernel_call(body, out_shapes, operands, scratch=(), micros=1.0, space=pltpu.VMEM, limit=20):
    vmem = pl.BlockSpec(memory_space=pltpu.VMEM)
    taken = pl.BlockSpec(memory_space=space)
    return pl.pallas_call(
        body,
        out_shape=out_shapes,
        in_specs=[taken] * len(operands),
        out_specs=[vmem] * len(out_shapes),
        scratch_shapes=list(scratch),
        compiler_params=pltpu.CompilerParams(vmem_limit_bytes=limit * 2**20),
        cost_estimate=pl.CostEstimate(flops=int(micros * 1e9), bytes_accessed=1, transcendentals=0),
    )(*operands)


def per_device(
    residual,
    cotangent,
    seq_lengths,
    gain_attn,
    shift_attn,
    gain_mlp,
    shift_mlp,
    w_qkv,
    b_qkv,
    w_out,
    b_out,
    w_up,
    b_up,
    w_down,
    b_down,
):
    places = lax.axis_size("dp")
    levels = places // PLANE
    plane_at = place()[0]
    own_rows, model = residual.shape
    slots = 2 * own_rows
    rows_all = PLANE * slots
    owned = w_up.shape[0]
    width = w_up.shape[1] // PLANE
    head_blocks = w_out.shape[0] // BLK
    columns = 4 * BLK + 2 * width
    direct = levels if levels == 4 and owned % 16 == 0 else 0
    level_groups = [[lev * PLANE + j for lev in range(levels)] for j in range(PLANE)]
    shape = jax.ShapeDtypeStruct

    def to_plane(x, k):
        return lax.ppermute(x, "dp", [(j, j ^ k) for j in range(places)])

    def to_level(x, m):
        return lax.ppermute(x, "dp", [(j, j ^ (m * PLANE)) for j in range(places)])

    def to_peer(x):
        return lax.ppermute(x, "tensor", [(0, 1), (1, 0)])

    passing = [(0, 2), (3, 1), (1, 0), (2, 3)]

    def to_pass(x, back=False):
        pairs = [(b, a) if back else (a, b) for a, b in passing]
        return lax.ppermute(x, "dp", [(a * PLANE + j, b * PLANE + j) for a, b in pairs for j in range(PLANE)])

    held = (w_qkv, w_out.T, w_up, w_down.T)
    shares = kernel_call(
        share_kernel,
        [shape((owned, columns), BF16)] * PLANE,
        held,
        scratch=[pltpu.VMEM(a.shape, a.dtype) for a in held] + [pltpu.SemaphoreType.DMA((4,))],
        space=pl.ANY,
        limit=63,
    )
    received = [to_plane(shares[k], k) for k in range(1, PLANE)]
    residual_m, cotangent_m, lengths_m, _ = lax.optimization_barrier((residual, cotangent, seq_lengths, shares))
    notes = jnp.pad(lengths_m.astype(BF16), ((0, NOTES - 1), (0, model - seq_lengths.shape[1])))
    message = jnp.concatenate([residual_m, cotangent_m, notes], axis=0)
    if direct:
        own = shares[0]
        own_near, own_far = to_level(own, 1), to_level(own, 3)
        others = kernel_call(join_kernel, [shape(((PLANE - 1) * owned, columns), BF16)], received, micros=20)[0]
        others, own, own_near, own_far, message = lax.optimization_barrier(
            (others, own, own_near, own_far, message)
        )
        near, far = to_level(others, 1), to_level(others, 3)
        own_mid = to_pass(kernel_call(choose_kernel, [shape(own.shape, BF16)], (own, own_far))[0])
    messages = [message] + [to_plane(message, k) for k in range(1, PLANE)]
    if direct:
        chosen = kernel_call(choose_kernel, [shape(others.shape, BF16)], (others, far), micros=20)[0]
        messages, own_mid, near, far, chosen = lax.optimization_barrier((messages, own_mid, near, far, chosen))
        mid = to_pass(chosen)
        pieces = [own, own_near, own_mid, own_far, others, near, mid, far]
    else:
        every = jnp.concatenate(xor_sorted([shares[0]] + received, plane_at), axis=0)
        pieces = [lax.all_gather(every, "dp", axis=0, tiled=True, axis_index_groups=level_groups)]
    rows = jnp.concatenate(messages, axis=0)
    params = jnp.stack([gain_attn, shift_attn, gain_mlp, shift_mlp] + [jnp.zeros_like(gain_attn)] * 4)
    x1, x2, xh, g, g_own, lengths, bo = kernel_call(
        rows_kernel,
        [shape((rows_all, model), BF16)] * 4
        + [shape((own_rows, model), BF16), shape((8, 128), F32), shape((1, model), F32)],
        (params, rows, to_peer(rows)),
        micros=4,
    )

    block_at = jnp.minimum(plane_at, head_blocks - 1) * BLK
    bias_heads = lax.dynamic_slice_in_dim(b_qkv, block_at, BLK, 1).reshape(1, 3 * BLK)
    bias_up = lax.dynamic_slice_in_dim(b_up, plane_at * width, width, 0).reshape(1, width)
    za, gp, gh, w, gb, *messages = kernel_call(
        partial(layer_kernel, direct),
        [
            shape((rows_all, BLK + width), BF16),
            shape((rows_all, 3 * BLK), BF16),
            shape((rows_all, width), BF16),
            shape((model, columns), BF16),
            shape((1, width + 3 * BLK), F32),
        ]
        + [shape((PLANE * owned if direct else model, columns), BF16)] * max(direct, 1),
        (lengths, x1, x2, g, bias_heads, bias_up, *rotary_tables(slots), *pieces),
        scratch=[pltpu.VMEM((model, columns), BF16)],
        micros=12,
        limit=30,
    )
    if direct:
        passed = to_pass(messages[2], back=True)
    keep, send = kernel_call(
        products_kernel,
        [shape((rows_all + NOTES, model), BF16)] * 2,
        (params, xh, w, za, gp, gh, gb, bo),
        scratch=[pltpu.VMEM((2, slots, model), F32)],
        micros=4,
    )
    from_peer = to_peer(send)
    extra, extra_shapes = (), []
    if direct:
        relayed = kernel_call(
            relay_kernel, [shape((PLANE * owned, columns), BF16)], (messages[3], passed), micros=20
        )[0]
        relayed, from_peer = lax.optimization_barrier((relayed, from_peer))
        extra = (messages[1], relayed)
        extra_shapes = [shape((PLANE * owned + NOTES, columns), BF16)] * 2
    laid = kernel_call(
        partial(pair_kernel, direct),
        extra_shapes + [shape((NOTES, model), BF16)] + [shape((slots, model), BF16)] * PLANE,
        (keep, from_peer, *extra),
        micros=2,
    )

    notes, outgoing = laid[-PLANE - 1], laid[-PLANE:]

    parts = [outgoing[0]] + [to_plane(outgoing[k], k) for k in range(1, PLANE)]
    if direct:
        near, far = to_level(laid[0], 1), to_level(laid[1], 3)
        notes_after, parts[1] = lax.optimization_barrier((notes, parts[1]))
        notes_mid = to_level(notes_after, 2)
        parts, near, far, notes_mid = lax.optimization_barrier((parts, near, far, notes_mid))
        backs = kernel_call(
            combine_kernel,
            [shape((owned + NOTES, columns), F32)] + [shape((owned + NOTES, columns), BF16)] * (PLANE - 1),
            (messages[0], near, passed, far, notes, notes_mid),
        )
    else:
        sums = lax.psum_scatter(
            messages[0], "dp", scatter_dimension=0, tiled=True, axis_index_groups=level_groups
        ).reshape(PLANE, owned, columns)
        notes = lax.all_gather(notes, "dp", axis=0, axis_index_groups=level_groups)
        notes = jnp.sum(notes.astype(F32), axis=0).astype(BF16)
        notes = jnp.concatenate([jnp.zeros((NOTES, columns - model), BF16), notes], axis=1)
        backs = [
            jnp.concatenate([lax.dynamic_index_in_dim(sums, plane_at ^ k, 0, keepdims=False), notes], axis=0)
            for k in range(PLANE)
        ]
    backs = [backs[0]] + [to_plane(backs[k], k) for k in range(1, PLANE)]
    result, grad_residual = kernel_call(
        rows_out_kernel,
        [shape((own_rows, model), BF16), shape((own_rows, model), F32)],
        (residual, g_own, b_out.reshape(1, model), b_down.reshape(1, model), *parts),
    )
    grad_up, grad_down, grad_qkv, grad_out_w, grad_b_up, grad_b_qkv, *common = kernel_call(
        owner_kernel,
        [
            shape((owned, PLANE * width), F32),
            shape((owned, PLANE * width), F32),
            shape((3, owned, head_blocks * BLK), F32),
            shape((owned, head_blocks * BLK), F32),
            shape((PLANE * width // BLK, BLK), F32),
            shape((3, head_blocks * BLK), F32),
        ]
        + [shape((model // BLK, BLK), F32)] * 6,
        backs,
    )
    common = [total.reshape(model) for total in common]
    return (
        result,
        grad_residual,
        *common[2:],
        grad_qkv,
        grad_b_qkv,
        grad_out_w.T,
        common[0],
        grad_up,
        grad_b_up.reshape(PLANE * width),
        grad_down.T,
        common[1],
    )


def solution(mesh):
    return jax.shard_map(
        per_device,
        mesh=mesh,
        in_specs=(
            P(("dp", "tensor"), None),
            P(("dp", "tensor"), None),
            P("dp", None),
            P(),
            P(),
            P(),
            P(),
            P(None, "dp", "tensor"),
            P(None, "tensor"),
            P("tensor", "dp"),
            P(),
            P("dp", "tensor"),
            P("tensor"),
            P("tensor", "dp"),
            P(),
        ),
        out_specs=(
            P(("dp", "tensor"), None),
            P(("dp", "tensor"), None),
            P(),
            P(),
            P(),
            P(),
            P(None, "dp", "tensor"),
            P(None, "tensor"),
            P("tensor", "dp"),
            P(),
            P("dp", "tensor"),
            P("tensor"),
            P("tensor", "dp"),
            P(),
        ),
        check_vma=False,
    )
```

```python
import math
from functools import partial

import jax
import jax.numpy as jnp
import numpy as np
from jax import lax
from jax.experimental import pallas as pl
from jax.experimental.pallas import tpu as pltpu
from jax.sharding import PartitionSpec as P

HD = 64
ROT = 16
PLANE = 4
BLK = 2 * HD
NOTES = 16
eps = 1e-05
F32 = jnp.float32
BF16 = jnp.bfloat16


def dot(a, b):
    return jnp.dot(a, b, preferred_element_type=F32)


def dot_nt(a, b):
    return lax.dot_general(a, b, (((1,), (1,)), ((), ())), preferred_element_type=F32)


def dot_tn(a, b):
    return lax.dot_general(a, b, (((0,), (0,)), ((), ())), preferred_element_type=F32)


def place():
    index = lax.axis_index("dp")
    return index % PLANE, index // PLANE


def is_inner():
    level = place()[1]
    return (level == 1) | (level == 2)


def xor_sorted(parts, index):
    parts = list(parts)
    bit = 1
    while bit < len(parts):
        swap = (index & bit) != 0
        parts = [jnp.where(swap, parts[j ^ bit], parts[j]) for j in range(len(parts))]
        bit *= 2
    return parts


def tree_sum(parts):
    parts = list(parts)
    while len(parts) > 1:
        parts = [parts[j] + parts[j + 1] for j in range(0, len(parts), 2)]
    return parts[0]


def rotary_tables(rows):
    half = ROT // 2
    inverse = np.float32(10000.0) ** (-np.arange(half, dtype=np.float32) * np.float32(2.0 / ROT))
    angle = np.arange(rows, dtype=np.float32)[:, None] * inverse.astype(np.float32)[None, :]
    cos, sin = np.cos(angle), np.sin(angle)
    rest = np.ones((rows, HD - ROT), np.float32)
    none = np.zeros((rows, half), np.float32)
    keep = np.concatenate([cos, cos, rest], axis=1)
    low = np.concatenate([-sin, none, 0.0 * rest], axis=1)
    high = np.concatenate([none, sin, 0.0 * rest], axis=1)
    return tuple(
        np.concatenate([t] * (BLK // HD), axis=1).astype(np.float32) for t in (keep, low, high)
    )


def share_kernel(*refs):
    whole_refs, share_refs = refs[:4], refs[4 : 4 + PLANE]
    held_refs, arrived = refs[4 + PLANE : -1], refs[-1]
    copies = [
        pltpu.make_async_copy(whole, held, arrived.at[j])
        for j, (whole, held) in enumerate(zip(whole_refs, held_refs))
    ]
    for copy in copies:
        copy.start()
    for copy in copies:
        copy.wait()
    qkv_ref, out_ref, up_ref, down_ref = held_refs
    head_blocks = out_ref.shape[1] // BLK
    width = up_ref.shape[1] // PLANE
    for k in range(PLANE):
        other = place()[0] ^ k
        heads, out = 3 * BLK, 3 * BLK + width
        at = pl.ds(pl.multiple_of(jnp.minimum(other, head_blocks - 1) * BLK, BLK), BLK)
        for c in range(4):
            block = qkv_ref[c, :, at] if c < 3 else out_ref[:, at]
            block = jnp.where(other < head_blocks, block.astype(F32), 0.0)
            start = c * BLK if c < 3 else out
            share_refs[k][:, start : start + BLK] = block.astype(BF16)
        at = pl.ds(pl.multiple_of(other * width, BLK), width)
        share_refs[k][:, heads:out] = up_ref[:, at]
        share_refs[k][:, out + BLK :] = down_ref[:, at]


def rows_at(m, k, owned):
    plane_at, level_at = place()
    return pl.ds(pl.multiple_of(((level_at ^ m) * PLANE + (plane_at ^ k)) * owned, owned), owned)


def rows_kernel(params_ref, own_ref, peer_ref, x1_ref, x2_ref, xh_ref, g_ref, g_own_ref, length_ref, bo_ref):
    half = lax.axis_index("tensor")
    own_rows = g_own_ref.shape[0]
    slots = 2 * own_rows
    params = params_ref[...]
    length_ref[...] = jnp.zeros_like(length_ref)
    for k in range(PLANE):
        start = k * (slots + NOTES)
        length = own_ref[start + slots : start + slots + NOTES, :].astype(F32)
        length = jnp.sum(length[0:1], axis=-1, keepdims=True)
        length_ref[k : k + 1, :] = jnp.broadcast_to(length, (1, length_ref.shape[1]))
        for which, ref in enumerate((own_ref, peer_ref)):
            part = half if which == 0 else 1 - half
            x = ref[start : start + own_rows, :].astype(F32)
            centre = jnp.mean(x, axis=-1, keepdims=True)
            off = x - centre
            spread = jnp.mean(off * off, axis=-1, keepdims=True)
            xh = off * lax.rsqrt(spread + eps)
            at = pl.ds(pl.multiple_of(k * slots + part * own_rows, own_rows), own_rows)
            x1_ref[at, :] = (xh * params[0:1] + params[1:2]).astype(BF16)
            x2_ref[at, :] = (xh * params[2:3] + params[3:4]).astype(BF16)
            xh_ref[at, :] = xh.astype(BF16)
            row = lax.broadcasted_iota(jnp.int32, (own_rows, 1), 0) + part * own_rows
            g = ref[start + own_rows : start + slots, :].astype(F32)
            g = jnp.where(row.astype(F32) < length, g, 0.0)
            g_ref[at, :] = g.astype(BF16)
            if k == 0 and which == 0:
                g_own_ref[...] = g.astype(BF16)
                bo_ref[...] = jnp.sum(g, axis=0, keepdims=True)


def layer_kernel(levels, *refs):
    length_ref, x1_ref, x2_ref, g_ref, bias_ref, bias_up_ref, keep_ref, low_ref, high_ref = refs[:9]
    pieces = refs[9 : 9 + (7 if levels else 1)]
    za_ref, gp_ref, gh_ref, w_ref, gb_ref = refs[9 + len(pieces) : 14 + len(pieces)]
    message_refs, gw_ref = refs[14 + len(pieces) : -1], refs[-1]
    if levels:
        owned = pieces[0].shape[0]
        for own, others, m in ((0, 3, 0), (1, 4, 1), (2, 5, 3)):
            w_ref[rows_at(m, 0, owned), :] = pieces[own][...]
            for k in range(1, PLANE):
                w_ref[rows_at(m, k, owned), :] = pieces[others][(k - 1) * owned : k * owned, :]
        for k in range(PLANE):
            w_ref[rows_at(2, k, owned), :] = pieces[6][k * owned : (k + 1) * owned, :]
    else:
        w_ref[...] = pieces[0][...]
        gw_ref = message_refs[0]
    width = bias_up_ref.shape[1]
    heads, out = 3 * BLK, 3 * BLK + width
    slots = keep_ref.shape[0]
    keep, low, high = keep_ref[...], low_ref[...], high_ref[...]

    def turn(x, sign):
        return x * keep + sign * (
            pltpu.roll(x, BLK - ROT // 2, 1) * low + pltpu.roll(x, ROT // 2, 1) * high
        )

    lane = lax.broadcasted_iota(jnp.int32, (slots, BLK), 1)
    first = lane < HD
    q_row = lax.broadcasted_iota(jnp.int32, (2 * slots, slots), 0) & (slots - 1)
    k_row = lax.broadcasted_iota(jnp.int32, (2 * slots, slots), 1)

    def stacked(x):
        zero = jnp.zeros_like(x)
        return jnp.concatenate([jnp.where(first, x, zero), jnp.where(first, zero, x)], axis=0)

    def joined(x):
        return jnp.where(first, x[:slots], x[slots:])

    total = jnp.zeros((1, 3 * BLK), F32)
    total_up = jnp.zeros((1, width), F32)
    for k in range(PLANE):
        at = pl.ds(k * slots, slots)
        proj = dot(x1_ref[at, :], w_ref[:, :heads]) + bias_ref[...]
        hidden = dot(x2_ref[at, :], w_ref[:, heads:out]) + bias_up_ref[...]
        back = dot(g_ref[at, :], w_ref[:, out:])
        query = stacked((turn(proj[:, :BLK], 1.0) * HD**-0.5).astype(BF16))
        key = turn(proj[:, BLK : 2 * BLK], 1.0).astype(BF16)
        value = proj[:, 2 * BLK :].astype(BF16)
        ga = stacked(back[:, :BLK].astype(BF16))
        logits = dot_nt(query, key)
        live = k_row.astype(F32) < length_ref[k : k + 1, 0:1]
        allowed = (k_row <= q_row) & (live | (k_row == q_row))
        logits = jnp.where(allowed, logits, -1000000000.0)
        weights = jnp.exp(logits - jnp.max(logits, axis=-1, keepdims=True))
        probs = weights / jnp.sum(weights, axis=-1, keepdims=True)
        rounded = probs.astype(BF16)
        za_ref[at, :BLK] = joined(dot(rounded, value)).astype(BF16)
        grad_probs = dot_nt(ga, value)
        inner = jnp.sum(probs * grad_probs, axis=-1, keepdims=True)
        grad_logits = (probs * (grad_probs - inner)).astype(BF16)
        grad_query = joined(dot(grad_logits, key)) * HD**-0.5
        grad_key = dot_tn(grad_logits, query)
        grad_value = dot_tn(rounded, ga)
        gp = jnp.concatenate([turn(grad_query, -1.0), turn(grad_key, -1.0), grad_value], axis=1).astype(BF16)
        gp_ref[at, :] = gp
        total = total + jnp.sum(gp.astype(F32), axis=0, keepdims=True)
        part = 0.5 + 0.5 * lax.erf(hidden * (0.5**0.5))
        za_ref[at, BLK:] = (hidden * part).astype(BF16)
        slope = part + hidden * jnp.exp(-0.5 * hidden * hidden) * (2.0 * math.pi) ** -0.5
        gh = (back[:, BLK:] * slope).astype(BF16)
        gh_ref[at, :] = gh
        total_up = total_up + jnp.sum(gh.astype(F32), axis=0, keepdims=True)
    gb_ref[:, :width] = total_up
    gb_ref[:, width:] = total
    gw_ref[:, :heads] = dot_tn(x1_ref[...], gp_ref[...]).astype(BF16)
    gw_ref[:, heads:out] = dot_tn(x2_ref[...], gh_ref[...]).astype(BF16)
    gw_ref[:, out:] = dot_tn(g_ref[...], za_ref[...]).astype(BF16)
    if levels:
        for m in range(levels):
            for k in range(PLANE):
                message_refs[m][k * owned : (k + 1) * owned, :] = gw_ref[rows_at(m, k, owned), :]


def products_kernel(
    params_ref, xh_ref, w_ref, za_ref, gp_ref, gh_ref, gb_ref, bo_ref, keep_ref, send_ref, notes_ref, stage_ref
):
    half = lax.axis_index("tensor")
    slots = stage_ref.shape[1]
    own_rows = slots // 2
    heads, out = 3 * BLK, 3 * BLK + gh_ref.shape[1]
    params = params_ref[...]
    gain1, gain2 = params[0:1], params[2:3]
    sums = [jnp.zeros((1, xh_ref.shape[1]), F32) for _ in range(4)]
    for k in range(PLANE):
        at = pl.ds(k * slots, slots)
        stage_ref[0] = dot_nt(za_ref[at, :], w_ref[:, out:])
        g1 = dot_nt(gp_ref[at, :], w_ref[:, :heads])
        g2 = dot_nt(gh_ref[at, :], w_ref[:, heads:out])
        stage_ref[1] = gain1 * g1 + gain2 * g2
        xh = xh_ref[at, :].astype(F32)
        for j, term in enumerate((g1 * xh, g1, g2 * xh, g2)):
            sums[j] = sums[j] + jnp.sum(term, axis=0, keepdims=True)
        mine = pl.ds(pl.multiple_of(half * own_rows, own_rows), own_rows)
        other = pl.ds(pl.multiple_of((1 - half) * own_rows, own_rows), own_rows)
        for j in range(2):
            to = pl.ds(k * slots + j * own_rows, own_rows)
            keep_ref[to, :] = stage_ref[j, mine, :].astype(BF16)
            send_ref[to, :] = stage_ref[j, other, :].astype(BF16)
    zero = jnp.zeros((NOTES - 6, xh_ref.shape[1]), F32)
    notes_ref[...] = jnp.concatenate([gb_ref[...], bo_ref[...]] + sums + [zero], axis=0).astype(BF16)


def join_kernel(*refs):
    owned = refs[0].shape[0]
    for k, ref in enumerate(refs[:-1]):
        refs[-1][k * owned : (k + 1) * owned, :] = ref[...]


def choose_kernel(own_ref, own_far_ref, others_ref, far_ref, out_ref):
    owned = own_ref.shape[0]
    for at, mine, afar in ((0, own_ref, own_far_ref), (owned, others_ref, far_ref)):
        rows = pl.ds(at, mine.shape[0])
        out_ref[rows, :] = jnp.where(is_inner(), afar[...].astype(F32), mine[...].astype(F32)).astype(BF16)


def relay_kernel(far_ref, passed_ref, out_ref):
    passed = jnp.where(is_inner(), passed_ref[...].astype(F32), 0.0)
    out_ref[...] = (far_ref[...].astype(F32) + passed).astype(BF16)


def pair_kernel(keep_ref, peer_ref, *refs):
    note_refs, out_refs = refs[:-PLANE], refs[-PLANE:]
    slots = out_refs[0].shape[0] - NOTES
    notes = tree_sum([ref[...].astype(F32) for ref in note_refs]).astype(BF16)
    for k, out_ref in enumerate(out_refs):
        at = pl.ds(k * slots, slots)
        out_ref[:slots, :] = (keep_ref[at, :].astype(F32) + peer_ref[at, :].astype(F32)).astype(BF16)
        out_ref[slots:, :] = notes


def rows_out_kernel(residual_ref, g_ref, b_out_ref, b_down_ref, *refs):
    part_refs, (result_ref, grad_ref, notes_ref) = refs[:PLANE], refs[PLANE:]
    own_rows = residual_ref.shape[0]
    slots = 2 * own_rows
    branch = tree_sum([ref[:own_rows, :].astype(F32) for ref in part_refs])
    x = residual_ref[...].astype(F32)
    result_ref[...] = (x + (branch + b_out_ref[...] + b_down_ref[...])).astype(BF16)
    off = x - jnp.mean(x, axis=-1, keepdims=True)
    scale = lax.rsqrt(jnp.mean(off * off, axis=-1, keepdims=True) + eps)
    xh = off * scale
    grad = tree_sum([ref[own_rows:slots, :].astype(F32) for ref in part_refs])
    grad = grad - jnp.mean(grad, axis=-1, keepdims=True) - xh * jnp.mean(grad * xh, axis=-1, keepdims=True)
    grad_ref[...] = g_ref[...].astype(F32) + scale * grad
    notes = [ref[slots:, :].astype(F32) for ref in part_refs]
    zero = jnp.zeros((NOTES - PLANE - 5, x.shape[1]), F32)
    notes = jnp.concatenate([note[0:1] for note in notes] + [tree_sum(notes)[1:6], zero], axis=0)
    notes_ref[...] = notes


def combine_kernel(own_ref, near_ref, passed_ref, far_ref, *out_refs):
    owned = own_ref.shape[0] // PLANE
    passed_here = jnp.logical_not(is_inner())
    for k, out_ref in enumerate(out_refs):
        at = pl.ds(k * owned, owned)
        total = own_ref[at, :].astype(F32) + near_ref[at, :].astype(F32) + far_ref[at, :].astype(F32)
        total = total + jnp.where(passed_here, passed_ref[at, :].astype(F32), 0.0)
        out_ref[...] = total.astype(out_ref.dtype)


def owner_kernel(*refs):
    part_refs, (notes_ref, peer_notes_ref) = refs[:PLANE], refs[PLANE:-12]
    up_ref, down_ref, qkv_ref, out_ref, b_up_ref, b_qkv_ref = refs[-12:-6]
    common_refs = refs[-6:]
    width = up_ref.shape[1] // PLANE
    head_blocks = out_ref.shape[1] // BLK
    heads, out = 3 * BLK, 3 * BLK + width
    notes = notes_ref[...]
    common = notes + peer_notes_ref[...]
    for k, part_ref in enumerate(part_refs):
        other = place()[0] ^ k
        at = pl.ds(pl.multiple_of(other * width, BLK), width)
        up_ref[:, at] = part_ref[:, heads:out].astype(F32)
        down_ref[:, at] = part_ref[:, out + BLK :].astype(F32)
        for j in range(width // BLK):
            b_up_ref[pl.ds(other * (width // BLK) + j, 1), :] = notes[k : k + 1, j * BLK : (j + 1) * BLK]

        @pl.when(other < head_blocks)
        def _():
            at = pl.ds(pl.multiple_of(other * BLK, BLK), BLK)
            for c in range(3):
                qkv_ref[c, :, at] = part_ref[:, c * BLK : (c + 1) * BLK].astype(F32)
                b_qkv_ref[c : c + 1, at] = notes[k : k + 1, width + c * BLK : width + (c + 1) * BLK]
            out_ref[:, at] = part_ref[:, out : out + BLK].astype(F32)

    for row, common_ref in zip((0, 0, 1, 2, 3, 4), common_refs):
        row = PLANE + row
        for j in range(common_ref.shape[0]):
            common_ref[j : j + 1, :] = common[row : row + 1, j * BLK : (j + 1) * BLK]


def kernel_call(body, out_shapes, operands, scratch=(), micros=1.0, space=pltpu.VMEM, limit=20):
    vmem = pl.BlockSpec(memory_space=pltpu.VMEM)
    taken = pl.BlockSpec(memory_space=space)
    return pl.pallas_call(
        body,
        out_shape=out_shapes,
        in_specs=[taken] * len(operands),
        out_specs=[vmem] * len(out_shapes),
        scratch_shapes=list(scratch),
        compiler_params=pltpu.CompilerParams(vmem_limit_bytes=limit * 2**20),
        cost_estimate=pl.CostEstimate(flops=int(micros * 1e9), bytes_accessed=1, transcendentals=0),
    )(*operands)


def per_device(
    residual,
    cotangent,
    seq_lengths,
    gain_attn,
    shift_attn,
    gain_mlp,
    shift_mlp,
    w_qkv,
    b_qkv,
    w_out,
    b_out,
    w_up,
    b_up,
    w_down,
    b_down,
):
    places = lax.axis_size("dp")
    levels = places // PLANE
    plane_at = place()[0]
    own_rows, model = residual.shape
    slots = 2 * own_rows
    rows_all = PLANE * slots
    owned = w_up.shape[0]
    width = w_up.shape[1] // PLANE
    head_blocks = w_out.shape[0] // BLK
    columns = 4 * BLK + 2 * width
    direct = levels if levels == 4 and owned % 16 == 0 else 0
    level_groups = [[lev * PLANE + j for lev in range(levels)] for j in range(PLANE)]
    shape = jax.ShapeDtypeStruct

    def to_plane(x, k):
        return lax.ppermute(x, "dp", [(j, j ^ k) for j in range(places)])

    def to_level(x, m):
        return lax.ppermute(x, "dp", [(j, j ^ (m * PLANE)) for j in range(places)])

    def to_peer(x):
        return lax.ppermute(x, "tensor", [(0, 1), (1, 0)])

    passing = [(0, 2), (3, 1), (1, 0), (2, 3)]

    def to_pass(x, back=False):
        pairs = [(b, a) if back else (a, b) for a, b in passing]
        return lax.ppermute(x, "dp", [(a * PLANE + j, b * PLANE + j) for a, b in pairs for j in range(PLANE)])

    held = (w_qkv, w_out.T, w_up, w_down.T)
    shares = kernel_call(
        share_kernel,
        [shape((owned, columns), BF16)] * PLANE,
        held,
        scratch=[pltpu.VMEM(a.shape, a.dtype) for a in held] + [pltpu.SemaphoreType.DMA((4,))],
        space=pl.ANY,
        limit=63,
    )
    received = [to_plane(shares[k], k) for k in range(1, PLANE)]
    residual_m, cotangent_m, lengths_m, _ = lax.optimization_barrier((residual, cotangent, seq_lengths, shares))
    notes = jnp.pad(lengths_m.astype(BF16), ((0, NOTES - 1), (0, model - seq_lengths.shape[1])))
    message = jnp.concatenate([residual_m, cotangent_m, notes], axis=0)
    if direct:
        own = shares[0]
        own_near, own_far = to_level(own, 1), to_level(own, 3)
        others = kernel_call(join_kernel, [shape(((PLANE - 1) * owned, columns), BF16)], received, micros=20)[0]
        others, message = lax.optimization_barrier((others, message))
        near, far = to_level(others, 1), to_level(others, 3)
        near, far = lax.optimization_barrier((near, far))
        message, own_near, own_far = lax.optimization_barrier((message, own_near, own_far))
        chosen = kernel_call(
            choose_kernel,
            [shape((PLANE * owned, columns), BF16)],
            (own, own_far, others, far),
            micros=20,
        )[0]
    messages = [message] + [to_plane(message, k) for k in range(1, PLANE)]
    if direct:
        pieces = [own, own_near, own_far, others, near, far, to_pass(chosen)]
    else:
        every = jnp.concatenate(xor_sorted([shares[0]] + received, plane_at), axis=0)
        pieces = [lax.all_gather(every, "dp", axis=0, tiled=True, axis_index_groups=level_groups)]
    rows = jnp.concatenate(messages, axis=0)
    params = jnp.stack([gain_attn, shift_attn, gain_mlp, shift_mlp] + [jnp.zeros_like(gain_attn)] * 4)
    x1, x2, xh, g, g_own, lengths, bo = kernel_call(
        rows_kernel,
        [shape((rows_all, model), BF16)] * 4
        + [shape((own_rows, model), BF16), shape((8, 128), F32), shape((1, model), F32)],
        (params, rows, to_peer(rows)),
        micros=1,
    )

    block_at = jnp.minimum(plane_at, head_blocks - 1) * BLK
    bias_heads = lax.dynamic_slice_in_dim(b_qkv, block_at, BLK, 1).reshape(1, 3 * BLK)
    bias_up = lax.dynamic_slice_in_dim(b_up, plane_at * width, width, 0).reshape(1, width)
    za, gp, gh, w, gb, *messages = kernel_call(
        partial(layer_kernel, direct),
        [
            shape((rows_all, BLK + width), BF16),
            shape((rows_all, 3 * BLK), BF16),
            shape((rows_all, width), BF16),
            shape((model, columns), BF16),
            shape((1, width + 3 * BLK), F32),
        ]
        + [shape((PLANE * owned if direct else model, columns), BF16)] * max(direct, 1),
        (lengths, x1, x2, g, bias_heads, bias_up, *rotary_tables(slots), *pieces),
        scratch=[pltpu.VMEM((model, columns), BF16)],
        micros=12,
        limit=30,
    )
    if direct:
        passed = to_pass(messages[2], back=True)
    keep, send, notes = kernel_call(
        products_kernel,
        [shape((rows_all, model), BF16)] * 2 + [shape((NOTES, model), BF16)],
        (params, xh, w, za, gp, gh, gb, bo),
        scratch=[pltpu.VMEM((2, slots, model), F32)],
        micros=4,
    )
    from_peer = to_peer(send)
    if direct:
        notes = [notes] + [to_level(notes, m) for m in range(1, levels)]
        relayed = kernel_call(
            relay_kernel, [shape((PLANE * owned, columns), BF16)], (messages[3], passed), micros=20
        )[0]
        relayed, from_peer, messages = lax.optimization_barrier((relayed, from_peer, messages))
    else:
        notes = lax.all_gather(notes, "dp", axis=0, axis_index_groups=level_groups)
        notes = [jnp.sum(notes.astype(F32), axis=0)]
    outgoing = kernel_call(
        pair_kernel,
        [shape((slots + NOTES, model), BF16)] * PLANE,
        (keep, from_peer, *notes),
        micros=2,
    )
    parts = [outgoing[0]] + [to_plane(outgoing[k], k) for k in range(1, PLANE)]

    if direct:
        near, far = to_level(messages[1], 1), to_level(relayed, 3)
        parts, near, far = lax.optimization_barrier((parts, near, far))
        backs = kernel_call(
            combine_kernel,
            [shape((owned, columns), F32)] + [shape((owned, columns), BF16)] * (PLANE - 1),
            (messages[0], near, passed, far),
        )
    else:
        sums = lax.psum_scatter(
            messages[0], "dp", scatter_dimension=0, tiled=True, axis_index_groups=level_groups
        ).reshape(PLANE, owned, columns)
        backs = [lax.dynamic_index_in_dim(sums, plane_at ^ k, 0, keepdims=False) for k in range(PLANE)]
    backs = [backs[0]] + [to_plane(backs[k], k) for k in range(1, PLANE)]
    result, grad_residual, notes = kernel_call(
        rows_out_kernel,
        [shape((own_rows, model), BF16), shape((own_rows, model), F32), shape((NOTES, model), F32)],
        (residual, g_own, b_out.reshape(1, model), b_down.reshape(1, model), *parts),
    )
    grad_up, grad_down, grad_qkv, grad_out_w, grad_b_up, grad_b_qkv, *common = kernel_call(
        owner_kernel,
        [
            shape((owned, PLANE * width), F32),
            shape((owned, PLANE * width), F32),
            shape((3, owned, head_blocks * BLK), F32),
            shape((owned, head_blocks * BLK), F32),
            shape((PLANE * width // BLK, BLK), F32),
            shape((3, head_blocks * BLK), F32),
        ]
        + [shape((model // BLK, BLK), F32)] * 6,
        (*backs, notes, to_peer(notes)),
    )
    common = [total.reshape(model) for total in common]
    return (
        result,
        grad_residual,
        *common[2:],
        grad_qkv,
        grad_b_qkv,
        grad_out_w.T,
        common[0],
        grad_up,
        grad_b_up.reshape(PLANE * width),
        grad_down.T,
        common[1],
    )


def solution(mesh):
    return jax.shard_map(
        per_device,
        mesh=mesh,
        in_specs=(
            P(("dp", "tensor"), None),
            P(("dp", "tensor"), None),
            P("dp", None),
            P(),
            P(),
            P(),
            P(),
            P(None, "dp", "tensor"),
            P(None, "tensor"),
            P("tensor", "dp"),
            P(),
            P("dp", "tensor"),
            P("tensor"),
            P("tensor", "dp"),
            P(),
        ),
        out_specs=(
            P(("dp", "tensor"), None),
            P(("dp", "tensor"), None),
            P(),
            P(),
            P(),
            P(),
            P(None, "dp", "tensor"),
            P(None, "tensor"),
            P("tensor", "dp"),
            P(),
            P("dp", "tensor"),
            P("tensor"),
            P("tensor", "dp"),
            P(),
        ),
        check_vma=False,
    )
```

```python
import math
from functools import partial

import jax
import jax.numpy as jnp
import numpy as np
from jax import lax
from jax.experimental import pallas as pl
from jax.experimental.pallas import tpu as pltpu
from jax.sharding import PartitionSpec as P

HD = 64
ROT = 16
PLANE = 4
BLK = 2 * HD
NOTES = 16
MARK = 16384.0
eps = 1e-05
F32 = jnp.float32
BF16 = jnp.bfloat16


def dot(a, b):
    return jnp.dot(a, b, preferred_element_type=F32)


def dot_nt(a, b):
    return lax.dot_general(a, b, (((1,), (1,)), ((), ())), preferred_element_type=F32)


def dot_tn(a, b):
    return lax.dot_general(a, b, (((0,), (0,)), ((), ())), preferred_element_type=F32)


def place():
    index = lax.axis_index("dp")
    return index % PLANE, index // PLANE


def is_inner():
    level = place()[1]
    return (level == 1) | (level == 2)


def xor_sorted(parts, index):
    parts = list(parts)
    bit = 1
    while bit < len(parts):
        swap = (index & bit) != 0
        parts = [jnp.where(swap, parts[j ^ bit], parts[j]) for j in range(len(parts))]
        bit *= 2
    return parts


def tree_sum(parts):
    parts = list(parts)
    while len(parts) > 1:
        parts = [parts[j] + parts[j + 1] for j in range(0, len(parts), 2)]
    return parts[0]


def rotary_tables(rows):
    half = ROT // 2
    inverse = np.float32(10000.0) ** (-np.arange(half, dtype=np.float32) * np.float32(2.0 / ROT))
    angle = np.arange(rows, dtype=np.float32)[:, None] * inverse.astype(np.float32)[None, :]
    cos, sin = np.cos(angle), np.sin(angle)
    rest = np.ones((rows, HD - ROT), np.float32)
    none = np.zeros((rows, half), np.float32)
    keep = np.concatenate([cos, cos, rest], axis=1)
    low = np.concatenate([-sin, none, 0.0 * rest], axis=1)
    high = np.concatenate([none, sin, 0.0 * rest], axis=1)
    return tuple(
        np.concatenate([t] * (BLK // HD), axis=1).astype(np.float32) for t in (keep, low, high)
    )


def share_kernel(*refs):
    whole_refs, share_refs = refs[:4], refs[4 : 4 + PLANE]
    held_refs, arrived = refs[4 + PLANE : -1], refs[-1]
    copies = [
        pltpu.make_async_copy(whole, held, arrived.at[j])
        for j, (whole, held) in enumerate(zip(whole_refs, held_refs))
    ]
    for copy in copies:
        copy.start()
    for copy in copies:
        copy.wait()
    qkv_ref, out_ref, up_ref, down_ref = held_refs
    head_blocks = out_ref.shape[1] // BLK
    width = up_ref.shape[1] // PLANE
    for k in range(PLANE):
        other = place()[0] ^ k
        heads, out = 3 * BLK, 3 * BLK + width
        at = pl.ds(pl.multiple_of(jnp.minimum(other, head_blocks - 1) * BLK, BLK), BLK)
        for c in range(4):
            block = qkv_ref[c, :, at] if c < 3 else out_ref[:, at]
            block = jnp.where(other < head_blocks, block.astype(F32), 0.0)
            start = c * BLK if c < 3 else out
            share_refs[k][:, start : start + BLK] = block.astype(BF16)
        at = pl.ds(pl.multiple_of(other * width, BLK), width)
        share_refs[k][:, heads:out] = up_ref[:, at]
        share_refs[k][:, out + BLK :] = down_ref[:, at]


def rows_at(m, k, owned):
    plane_at, level_at = place()
    return pl.ds(pl.multiple_of(((level_at ^ m) * PLANE + (plane_at ^ k)) * owned, owned), owned)


def rows_kernel(params_ref, own_ref, peer_ref, x1_ref, x2_ref, xh_ref, g_ref, g_own_ref, length_ref, bo_ref):
    half = lax.axis_index("tensor")
    own_rows = g_own_ref.shape[0]
    slots = 2 * own_rows
    params = params_ref[...]
    length_ref[...] = jnp.zeros_like(length_ref)
    for k in range(PLANE):
        start = k * slots
        count = jnp.zeros((1, 1), F32)
        for which, ref in enumerate((own_ref, peer_ref)):
            part = half if which == 0 else 1 - half
            x = ref[start : start + own_rows, :].astype(F32)
            centre = jnp.mean(x, axis=-1, keepdims=True)
            off = x - centre
            spread = jnp.mean(off * off, axis=-1, keepdims=True)
            xh = off * lax.rsqrt(spread + eps)
            at = pl.ds(pl.multiple_of(k * slots + part * own_rows, own_rows), own_rows)
            x1_ref[at, :] = (xh * params[0:1] + params[1:2]).astype(BF16)
            x2_ref[at, :] = (xh * params[2:3] + params[3:4]).astype(BF16)
            xh_ref[at, :] = xh.astype(BF16)
            g = ref[start + own_rows : start + slots, :].astype(F32)
            live = g[:, 0:1] < 0.5 * MARK
            count = count + jnp.sum(jnp.where(live, 1.0, 0.0), axis=0, keepdims=True)
            g = jnp.where(live, g, 0.0)
            g_ref[at, :] = g.astype(BF16)
            if k == 0 and which == 0:
                g_own_ref[...] = g.astype(BF16)
                bo_ref[...] = jnp.sum(g, axis=0, keepdims=True)
        length_ref[k : k + 1, :] = jnp.broadcast_to(count, (1, length_ref.shape[1]))


def layer_kernel(levels, *refs):
    length_ref, x1_ref, x2_ref, g_ref, bias_ref, bias_up_ref, keep_ref, low_ref, high_ref = refs[:9]
    pieces = refs[9 : 9 + (5 if levels else 1)]
    za_ref, gp_ref, gh_ref, w_ref, gb_ref = refs[9 + len(pieces) : 14 + len(pieces)]
    message_refs, gw_ref = refs[14 + len(pieces) : -1], refs[-1]
    if levels:
        owned = pieces[3].shape[0]
        for m in range(3):
            for k in range(PLANE):
                w_ref[rows_at(m, k, owned), :] = pieces[m][k * owned : (k + 1) * owned, :]
        w_ref[rows_at(3, 0, owned), :] = pieces[3][...]
        for k in range(1, PLANE):
            w_ref[rows_at(3, k, owned), :] = pieces[4][(k - 1) * owned : k * owned, :]
    else:
        w_ref[...] = pieces[0][...]
        gw_ref = message_refs[0]
    width = bias_up_ref.shape[1]
    heads, out = 3 * BLK, 3 * BLK + width
    slots = keep_ref.shape[0]
    keep, low, high = keep_ref[...], low_ref[...], high_ref[...]

    def turn(x, sign):
        return x * keep + sign * (
            pltpu.roll(x, BLK - ROT // 2, 1) * low + pltpu.roll(x, ROT // 2, 1) * high
        )

    lane = lax.broadcasted_iota(jnp.int32, (slots, BLK), 1)
    first = lane < HD
    q_row = lax.broadcasted_iota(jnp.int32, (2 * slots, slots), 0) & (slots - 1)
    k_row = lax.broadcasted_iota(jnp.int32, (2 * slots, slots), 1)

    def stacked(x):
        zero = jnp.zeros_like(x)
        return jnp.concatenate([jnp.where(first, x, zero), jnp.where(first, zero, x)], axis=0)

    def joined(x):
        return jnp.where(first, x[:slots], x[slots:])

    total = jnp.zeros((1, 3 * BLK), F32)
    total_up = jnp.zeros((1, width), F32)
    for k in range(PLANE):
        at = pl.ds(k * slots, slots)
        proj = dot(x1_ref[at, :], w_ref[:, :heads]) + bias_ref[...]
        hidden = dot(x2_ref[at, :], w_ref[:, heads:out]) + bias_up_ref[...]
        back = dot(g_ref[at, :], w_ref[:, out:])
        query = stacked((turn(proj[:, :BLK], 1.0) * HD**-0.5).astype(BF16))
        key = turn(proj[:, BLK : 2 * BLK], 1.0).astype(BF16)
        value = proj[:, 2 * BLK :].astype(BF16)
        ga = stacked(back[:, :BLK].astype(BF16))
        logits = dot_nt(query, key)
        live = k_row.astype(F32) < length_ref[k : k + 1, 0:1]
        allowed = (k_row <= q_row) & (live | (k_row == q_row))
        logits = jnp.where(allowed, logits, -1000000000.0)
        weights = jnp.exp(logits - jnp.max(logits, axis=-1, keepdims=True))
        probs = weights / jnp.sum(weights, axis=-1, keepdims=True)
        rounded = probs.astype(BF16)
        za_ref[at, :BLK] = joined(dot(rounded, value)).astype(BF16)
        grad_probs = dot_nt(ga, value)
        inner = jnp.sum(probs * grad_probs, axis=-1, keepdims=True)
        grad_logits = (probs * (grad_probs - inner)).astype(BF16)
        grad_query = joined(dot(grad_logits, key)) * HD**-0.5
        grad_key = dot_tn(grad_logits, query)
        grad_value = dot_tn(rounded, ga)
        gp = jnp.concatenate([turn(grad_query, -1.0), turn(grad_key, -1.0), grad_value], axis=1).astype(BF16)
        gp_ref[at, :] = gp
        total = total + jnp.sum(gp.astype(F32), axis=0, keepdims=True)
        part = 0.5 + 0.5 * lax.erf(hidden * (0.5**0.5))
        za_ref[at, BLK:] = (hidden * part).astype(BF16)
        slope = part + hidden * jnp.exp(-0.5 * hidden * hidden) * (2.0 * math.pi) ** -0.5
        gh = (back[:, BLK:] * slope).astype(BF16)
        gh_ref[at, :] = gh
        total_up = total_up + jnp.sum(gh.astype(F32), axis=0, keepdims=True)
    gb_ref[:, :width] = total_up
    gb_ref[:, width:] = total
    gw_ref[:, :heads] = dot_tn(x1_ref[...], gp_ref[...]).astype(BF16)
    gw_ref[:, heads:out] = dot_tn(x2_ref[...], gh_ref[...]).astype(BF16)
    gw_ref[:, out:] = dot_tn(g_ref[...], za_ref[...]).astype(BF16)
    if levels:
        for m in range(levels):
            for k in range(PLANE):
                message_refs[m][k * owned : (k + 1) * owned, :] = gw_ref[rows_at(m, k, owned), :]


def products_kernel(
    params_ref, xh_ref, w_ref, za_ref, gp_ref, gh_ref, gb_ref, bo_ref, keep_ref, send_ref, notes_ref, stage_ref
):
    half = lax.axis_index("tensor")
    slots = stage_ref.shape[1]
    own_rows = slots // 2
    heads, out = 3 * BLK, 3 * BLK + gh_ref.shape[1]
    params = params_ref[...]
    gain1, gain2 = params[0:1], params[2:3]
    sums = [jnp.zeros((1, xh_ref.shape[1]), F32) for _ in range(4)]
    for k in range(PLANE):
        at = pl.ds(k * slots, slots)
        stage_ref[0] = dot_nt(za_ref[at, :], w_ref[:, out:])
        g1 = dot_nt(gp_ref[at, :], w_ref[:, :heads])
        g2 = dot_nt(gh_ref[at, :], w_ref[:, heads:out])
        stage_ref[1] = gain1 * g1 + gain2 * g2
        xh = xh_ref[at, :].astype(F32)
        for j, term in enumerate((g1 * xh, g1, g2 * xh, g2)):
            sums[j] = sums[j] + jnp.sum(term, axis=0, keepdims=True)
        mine = pl.ds(pl.multiple_of(half * own_rows, own_rows), own_rows)
        other = pl.ds(pl.multiple_of((1 - half) * own_rows, own_rows), own_rows)
        for j in range(2):
            to = pl.ds(k * slots + j * own_rows, own_rows)
            keep_ref[to, :] = stage_ref[j, mine, :].astype(BF16)
            send_ref[to, :] = stage_ref[j, other, :].astype(BF16)
    zero = jnp.zeros((NOTES - 6, xh_ref.shape[1]), F32)
    notes_ref[...] = jnp.concatenate([gb_ref[...], bo_ref[...]] + sums + [zero], axis=0).astype(BF16)


def join_kernel(*refs):
    part_refs, (every_ref, others_ref) = refs[:PLANE], refs[PLANE:]
    owned = part_refs[0].shape[0]
    for k, ref in enumerate(part_refs):
        every_ref[k * owned : (k + 1) * owned, :] = ref[...]
        if k:
            others_ref[(k - 1) * owned : k * owned, :] = ref[...]


def choose_kernel(own_ref, own_far_ref, others_ref, far_ref, out_ref):
    owned = own_ref.shape[0]
    for at, mine, afar in ((0, own_ref, own_far_ref), (owned, others_ref, far_ref)):
        rows = pl.ds(at, mine.shape[0])
        out_ref[rows, :] = jnp.where(is_inner(), afar[...].astype(F32), mine[...].astype(F32)).astype(BF16)


def relay_kernel(far_ref, passed_ref, out_ref):
    passed = jnp.where(is_inner(), passed_ref[...].astype(F32), 0.0)
    out_ref[...] = (far_ref[...].astype(F32) + passed).astype(BF16)


def pair_kernel(keep_ref, peer_ref, *refs):
    note_refs, out_refs = refs[:-PLANE], refs[-PLANE:]
    slots = out_refs[0].shape[0] - NOTES
    notes = tree_sum([ref[...].astype(F32) for ref in note_refs]).astype(BF16)
    for k, out_ref in enumerate(out_refs):
        at = pl.ds(k * slots, slots)
        out_ref[:slots, :] = (keep_ref[at, :].astype(F32) + peer_ref[at, :].astype(F32)).astype(BF16)
        out_ref[slots:, :] = notes


def rows_out_kernel(residual_ref, g_ref, b_out_ref, b_down_ref, *refs):
    part_refs, (result_ref, grad_ref, notes_ref) = refs[:PLANE], refs[PLANE:]
    own_rows = residual_ref.shape[0]
    slots = 2 * own_rows
    branch = tree_sum([ref[:own_rows, :].astype(F32) for ref in part_refs])
    x = residual_ref[...].astype(F32)
    result_ref[...] = (x + (branch + b_out_ref[...] + b_down_ref[...])).astype(BF16)
    off = x - jnp.mean(x, axis=-1, keepdims=True)
    scale = lax.rsqrt(jnp.mean(off * off, axis=-1, keepdims=True) + eps)
    xh = off * scale
    grad = tree_sum([ref[own_rows:slots, :].astype(F32) for ref in part_refs])
    grad = grad - jnp.mean(grad, axis=-1, keepdims=True) - xh * jnp.mean(grad * xh, axis=-1, keepdims=True)
    grad_ref[...] = g_ref[...].astype(F32) + scale * grad
    notes = [ref[slots:, :].astype(F32) for ref in part_refs]
    zero = jnp.zeros((NOTES - PLANE - 5, x.shape[1]), F32)
    notes = jnp.concatenate([note[0:1] for note in notes] + [tree_sum(notes)[1:6], zero], axis=0)
    notes_ref[...] = notes


def combine_kernel(own_ref, near_ref, passed_ref, far_ref, *out_refs):
    owned = own_ref.shape[0] // PLANE
    passed_here = jnp.logical_not(is_inner())
    for k, out_ref in enumerate(out_refs):
        at = pl.ds(k * owned, owned)
        total = own_ref[at, :].astype(F32) + near_ref[at, :].astype(F32) + far_ref[at, :].astype(F32)
        total = total + jnp.where(passed_here, passed_ref[at, :].astype(F32), 0.0)
        out_ref[...] = total.astype(out_ref.dtype)


def owner_kernel(*refs):
    part_refs, (notes_ref, peer_notes_ref) = refs[:PLANE], refs[PLANE:-12]
    up_ref, down_ref, qkv_ref, out_ref, b_up_ref, b_qkv_ref = refs[-12:-6]
    common_refs = refs[-6:]
    width = up_ref.shape[1] // PLANE
    head_blocks = out_ref.shape[1] // BLK
    heads, out = 3 * BLK, 3 * BLK + width
    notes = notes_ref[...]
    common = notes + peer_notes_ref[...]
    for k, part_ref in enumerate(part_refs):
        other = place()[0] ^ k
        at = pl.ds(pl.multiple_of(other * width, BLK), width)
        up_ref[:, at] = part_ref[:, heads:out].astype(F32)
        down_ref[:, at] = part_ref[:, out + BLK :].astype(F32)
        for j in range(width // BLK):
            b_up_ref[pl.ds(other * (width // BLK) + j, 1), :] = notes[k : k + 1, j * BLK : (j + 1) * BLK]

        @pl.when(other < head_blocks)
        def _():
            at = pl.ds(pl.multiple_of(other * BLK, BLK), BLK)
            for c in range(3):
                qkv_ref[c, :, at] = part_ref[:, c * BLK : (c + 1) * BLK].astype(F32)
                b_qkv_ref[c : c + 1, at] = notes[k : k + 1, width + c * BLK : width + (c + 1) * BLK]
            out_ref[:, at] = part_ref[:, out : out + BLK].astype(F32)

    for row, common_ref in zip((0, 0, 1, 2, 3, 4), common_refs):
        row = PLANE + row
        for j in range(common_ref.shape[0]):
            common_ref[j : j + 1, :] = common[row : row + 1, j * BLK : (j + 1) * BLK]


def kernel_call(body, out_shapes, operands, scratch=(), micros=1.0, space=pltpu.VMEM, limit=20):
    vmem = pl.BlockSpec(memory_space=pltpu.VMEM)
    taken = pl.BlockSpec(memory_space=space)
    return pl.pallas_call(
        body,
        out_shape=out_shapes,
        in_specs=[taken] * len(operands),
        out_specs=[vmem] * len(out_shapes),
        scratch_shapes=list(scratch),
        compiler_params=pltpu.CompilerParams(vmem_limit_bytes=limit * 2**20),
        cost_estimate=pl.CostEstimate(flops=int(micros * 1e9), bytes_accessed=1, transcendentals=0),
    )(*operands)


def per_device(
    residual,
    cotangent,
    seq_lengths,
    gain_attn,
    shift_attn,
    gain_mlp,
    shift_mlp,
    w_qkv,
    b_qkv,
    w_out,
    b_out,
    w_up,
    b_up,
    w_down,
    b_down,
):
    places = lax.axis_size("dp")
    levels = places // PLANE
    plane_at = place()[0]
    own_rows, model = residual.shape
    slots = 2 * own_rows
    rows_all = PLANE * slots
    owned = w_up.shape[0]
    width = w_up.shape[1] // PLANE
    head_blocks = w_out.shape[0] // BLK
    columns = 4 * BLK + 2 * width
    direct = levels if levels == 4 and owned % 16 == 0 else 0
    level_groups = [[lev * PLANE + j for lev in range(levels)] for j in range(PLANE)]
    shape = jax.ShapeDtypeStruct

    def to_plane(x, k):
        return lax.ppermute(x, "dp", [(j, j ^ k) for j in range(places)])

    def to_level(x, m):
        return lax.ppermute(x, "dp", [(j, j ^ (m * PLANE)) for j in range(places)])

    def to_peer(x):
        return lax.ppermute(x, "tensor", [(0, 1), (1, 0)])

    passing = [(0, 2), (3, 1), (1, 0), (2, 3)]

    def to_pass(x, back=False):
        pairs = [(b, a) if back else (a, b) for a, b in passing]
        return lax.ppermute(x, "dp", [(a * PLANE + j, b * PLANE + j) for a, b in pairs for j in range(PLANE)])

    held = (w_qkv, w_out.T, w_up, w_down.T)
    shares = kernel_call(
        share_kernel,
        [shape((owned, columns), BF16)] * PLANE,
        held,
        scratch=[pltpu.VMEM(a.shape, a.dtype) for a in held] + [pltpu.SemaphoreType.DMA((4,))],
        space=pl.ANY,
        limit=63,
    )
    received = [to_plane(shares[k], k) for k in range(1, PLANE)]
    residual_m, cotangent_m, lengths_m, _ = lax.optimization_barrier((residual, cotangent, seq_lengths, shares))
    row = lax.axis_index("tensor") * own_rows + jnp.arange(own_rows, dtype=jnp.int32)
    live = (row < jnp.sum(lengths_m[0]))[:, None]
    message = jnp.concatenate([residual_m, jnp.where(live, cotangent_m, jnp.asarray(MARK, BF16))], axis=0)
    if direct:
        own = shares[0]
        own_far = to_level(own, 3)
        every, others = kernel_call(
            join_kernel,
            [shape((PLANE * owned, columns), BF16), shape(((PLANE - 1) * owned, columns), BF16)],
            (own, *received),
            micros=20,
        )
        every, others, message = lax.optimization_barrier((every, others, message))
        near, far = to_level(every, 1), to_level(others, 3)
        near, far = lax.optimization_barrier((near, far))
        message, own_far = lax.optimization_barrier((message, own_far))
        chosen = kernel_call(
            choose_kernel,
            [shape((PLANE * owned, columns), BF16)],
            (own, own_far, others, far),
            micros=20,
        )[0]
    messages = [message] + [to_plane(message, k) for k in range(1, PLANE)]
    if direct:
        pieces = [every, near, to_pass(chosen), own_far, far]
    else:
        every = jnp.concatenate(xor_sorted([shares[0]] + received, plane_at), axis=0)
        pieces = [lax.all_gather(every, "dp", axis=0, tiled=True, axis_index_groups=level_groups)]
    rows = jnp.concatenate(messages, axis=0)
    params = jnp.stack([gain_attn, shift_attn, gain_mlp, shift_mlp] + [jnp.zeros_like(gain_attn)] * 4)
    x1, x2, xh, g, g_own, lengths, bo = kernel_call(
        rows_kernel,
        [shape((rows_all, model), BF16)] * 4
        + [shape((own_rows, model), BF16), shape((8, 128), F32), shape((1, model), F32)],
        (params, rows, to_peer(rows)),
        micros=1,
    )

    block_at = jnp.minimum(plane_at, head_blocks - 1) * BLK
    bias_heads = lax.dynamic_slice_in_dim(b_qkv, block_at, BLK, 1).reshape(1, 3 * BLK)
    bias_up = lax.dynamic_slice_in_dim(b_up, plane_at * width, width, 0).reshape(1, width)
    za, gp, gh, w, gb, *messages = kernel_call(
        partial(layer_kernel, direct),
        [
            shape((rows_all, BLK + width), BF16),
            shape((rows_all, 3 * BLK), BF16),
            shape((rows_all, width), BF16),
            shape((model, columns), BF16),
            shape((1, width + 3 * BLK), F32),
        ]
        + [shape((PLANE * owned if direct else model, columns), BF16)] * max(direct, 1),
        (lengths, x1, x2, g, bias_heads, bias_up, *rotary_tables(slots), *pieces),
        scratch=[pltpu.VMEM((model, columns), BF16)],
        micros=12,
        limit=30,
    )
    if direct:
        passed = to_pass(messages[2], back=True)
    keep, send, notes = kernel_call(
        products_kernel,
        [shape((rows_all, model), BF16)] * 2 + [shape((NOTES, model), BF16)],
        (params, xh, w, za, gp, gh, gb, bo),
        scratch=[pltpu.VMEM((2, slots, model), F32)],
        micros=4,
    )
    from_peer = to_peer(send)
    if direct:
        notes = [notes] + [to_level(notes, m) for m in range(1, levels)]
        relayed = kernel_call(
            relay_kernel, [shape((PLANE * owned, columns), BF16)], (messages[3], passed), micros=20
        )[0]
        relayed, from_peer, messages = lax.optimization_barrier((relayed, from_peer, messages))
    else:
        notes = lax.all_gather(notes, "dp", axis=0, axis_index_groups=level_groups)
        notes = [jnp.sum(notes.astype(F32), axis=0)]
    outgoing = kernel_call(
        pair_kernel,
        [shape((slots + NOTES, model), BF16)] * PLANE,
        (keep, from_peer, *notes),
        micros=2,
    )
    parts = [outgoing[0]] + [to_plane(outgoing[k], k) for k in range(1, PLANE)]

    if direct:
        near, far = to_level(messages[1], 1), to_level(relayed, 3)
        parts, near, far = lax.optimization_barrier((parts, near, far))
        backs = kernel_call(
            combine_kernel,
            [shape((owned, columns), F32)] + [shape((owned, columns), BF16)] * (PLANE - 1),
            (messages[0], near, passed, far),
        )
    else:
        sums = lax.psum_scatter(
            messages[0], "dp", scatter_dimension=0, tiled=True, axis_index_groups=level_groups
        ).reshape(PLANE, owned, columns)
        backs = [lax.dynamic_index_in_dim(sums, plane_at ^ k, 0, keepdims=False) for k in range(PLANE)]
    backs = [backs[0]] + [to_plane(backs[k], k) for k in range(1, PLANE)]
    result, grad_residual, notes = kernel_call(
        rows_out_kernel,
        [shape((own_rows, model), BF16), shape((own_rows, model), F32), shape((NOTES, model), F32)],
        (residual, g_own, b_out.reshape(1, model), b_down.reshape(1, model), *parts),
    )
    grad_up, grad_down, grad_qkv, grad_out_w, grad_b_up, grad_b_qkv, *common = kernel_call(
        owner_kernel,
        [
            shape((owned, PLANE * width), F32),
            shape((owned, PLANE * width), F32),
            shape((3, owned, head_blocks * BLK), F32),
            shape((owned, head_blocks * BLK), F32),
            shape((PLANE * width // BLK, BLK), F32),
            shape((3, head_blocks * BLK), F32),
        ]
        + [shape((model // BLK, BLK), F32)] * 6,
        (*backs, notes, to_peer(notes)),
    )
    common = [total.reshape(model) for total in common]
    return (
        result,
        grad_residual,
        *common[2:],
        grad_qkv,
        grad_b_qkv,
        grad_out_w.T,
        common[0],
        grad_up,
        grad_b_up.reshape(PLANE * width),
        grad_down.T,
        common[1],
    )


def solution(mesh):
    return jax.shard_map(
        per_device,
        mesh=mesh,
        in_specs=(
            P(("dp", "tensor"), None),
            P(("dp", "tensor"), None),
            P("dp", None),
            P(),
            P(),
            P(),
            P(),
            P(None, "dp", "tensor"),
            P(None, "tensor"),
            P("tensor", "dp"),
            P(),
            P("dp", "tensor"),
            P("tensor"),
            P("tensor", "dp"),
            P(),
        ),
        out_specs=(
            P(("dp", "tensor"), None),
            P(("dp", "tensor"), None),
            P(),
            P(),
            P(),
            P(),
            P(None, "dp", "tensor"),
            P(None, "tensor"),
            P("tensor", "dp"),
            P(),
            P("dp", "tensor"),
            P("tensor"),
            P("tensor", "dp"),
            P(),
        ),
        check_vma=False,
    )
```

```python
import math
from functools import partial

import jax
import jax.numpy as jnp
import numpy as np
from jax import lax
from jax.experimental import pallas as pl
from jax.experimental.pallas import tpu as pltpu
from jax.sharding import PartitionSpec as P

HD = 64
ROT = 16
PLANE = 4
BLK = 2 * HD
NOTES = 16
MARK = 16384.0
eps = 1e-05
F32 = jnp.float32
BF16 = jnp.bfloat16


def dot(a, b):
    return jnp.dot(a, b, preferred_element_type=F32)


def dot_nt(a, b):
    return lax.dot_general(a, b, (((1,), (1,)), ((), ())), preferred_element_type=F32)


def dot_tn(a, b):
    return lax.dot_general(a, b, (((0,), (0,)), ((), ())), preferred_element_type=F32)


def place():
    index = lax.axis_index("dp")
    return index % PLANE, index // PLANE


def is_inner():
    level = place()[1]
    return (level == 1) | (level == 2)


def xor_sorted(parts, index):
    parts = list(parts)
    bit = 1
    while bit < len(parts):
        swap = (index & bit) != 0
        parts = [jnp.where(swap, parts[j ^ bit], parts[j]) for j in range(len(parts))]
        bit *= 2
    return parts


def tree_sum(parts):
    parts = list(parts)
    while len(parts) > 1:
        parts = [parts[j] + parts[j + 1] for j in range(0, len(parts), 2)]
    return parts[0]


def rotary_tables(rows):
    half = ROT // 2
    inverse = np.float32(10000.0) ** (-np.arange(half, dtype=np.float32) * np.float32(2.0 / ROT))
    angle = np.arange(rows, dtype=np.float32)[:, None] * inverse.astype(np.float32)[None, :]
    cos, sin = np.cos(angle), np.sin(angle)
    rest = np.ones((rows, HD - ROT), np.float32)
    none = np.zeros((rows, half), np.float32)
    keep = np.concatenate([cos, cos, rest], axis=1)
    low = np.concatenate([-sin, none, 0.0 * rest], axis=1)
    high = np.concatenate([none, sin, 0.0 * rest], axis=1)
    return tuple(
        np.concatenate([t] * (BLK // HD), axis=1).astype(np.float32) for t in (keep, low, high)
    )


def share_kernel(*refs):
    whole_refs, share_refs = refs[:4], refs[4 : 4 + PLANE]
    held_refs, arrived = refs[4 + PLANE : -1], refs[-1]
    copies = [
        pltpu.make_async_copy(whole, held, arrived.at[j])
        for j, (whole, held) in enumerate(zip(whole_refs, held_refs))
    ]
    for copy in copies:
        copy.start()
    for copy in copies:
        copy.wait()
    qkv_ref, out_ref, up_ref, down_ref = held_refs
    head_blocks = out_ref.shape[1] // BLK
    width = up_ref.shape[1] // PLANE
    for k in range(PLANE):
        other = place()[0] ^ k
        heads, out = 3 * BLK, 3 * BLK + width
        at = pl.ds(pl.multiple_of(jnp.minimum(other, head_blocks - 1) * BLK, BLK), BLK)
        for c in range(4):
            block = qkv_ref[c, :, at] if c < 3 else out_ref[:, at]
            block = jnp.where(other < head_blocks, block.astype(F32), 0.0)
            start = c * BLK if c < 3 else out
            share_refs[k][:, start : start + BLK] = block.astype(BF16)
        at = pl.ds(pl.multiple_of(other * width, BLK), width)
        share_refs[k][:, heads:out] = up_ref[:, at]
        share_refs[k][:, out + BLK :] = down_ref[:, at]


def rows_at(m, k, owned):
    plane_at, level_at = place()
    return pl.ds(pl.multiple_of(((level_at ^ m) * PLANE + (plane_at ^ k)) * owned, owned), owned)


def rows_kernel(params_ref, own_ref, peer_ref, x1_ref, x2_ref, xh_ref, g_ref, g_own_ref, length_ref, bo_ref):
    half = lax.axis_index("tensor")
    own_rows = g_own_ref.shape[0]
    slots = 2 * own_rows
    params = params_ref[...]
    length_ref[...] = jnp.zeros_like(length_ref)
    for k in range(PLANE):
        start = k * slots
        count = jnp.zeros((1, 1), F32)
        for which, ref in enumerate((own_ref, peer_ref)):
            part = half if which == 0 else 1 - half
            x = ref[start : start + own_rows, :].astype(F32)
            centre = jnp.mean(x, axis=-1, keepdims=True)
            off = x - centre
            spread = jnp.mean(off * off, axis=-1, keepdims=True)
            xh = off * lax.rsqrt(spread + eps)
            at = pl.ds(pl.multiple_of(k * slots + part * own_rows, own_rows), own_rows)
            x1_ref[at, :] = (xh * params[0:1] + params[1:2]).astype(BF16)
            x2_ref[at, :] = (xh * params[2:3] + params[3:4]).astype(BF16)
            xh_ref[at, :] = xh.astype(BF16)
            g = ref[start + own_rows : start + slots, :].astype(F32)
            live = g[:, 0:1] < 0.5 * MARK
            count = count + jnp.sum(jnp.where(live, 1.0, 0.0), axis=0, keepdims=True)
            g = jnp.where(live, g, 0.0)
            g_ref[at, :] = g.astype(BF16)
            if k == 0 and which == 0:
                g_own_ref[...] = g.astype(BF16)
                bo_ref[...] = jnp.sum(g, axis=0, keepdims=True)
        length_ref[k : k + 1, :] = jnp.broadcast_to(count, (1, length_ref.shape[1]))


def layer_kernel(levels, *refs):
    length_ref, x1_ref, x2_ref, g_ref, bias_ref, bias_up_ref, keep_ref, low_ref, high_ref = refs[:9]
    pieces = refs[9 : 9 + (5 if levels else 1)]
    za_ref, gp_ref, gh_ref, w_ref, gb_ref = refs[9 + len(pieces) : 14 + len(pieces)]
    message_refs, gw_ref = refs[14 + len(pieces) : -1], refs[-1]
    if levels:
        owned = pieces[3].shape[0]
        for m in range(3):
            for k in range(PLANE):
                w_ref[rows_at(m, k, owned), :] = pieces[m][k * owned : (k + 1) * owned, :]
        w_ref[rows_at(3, 0, owned), :] = pieces[3][...]
        for k in range(1, PLANE):
            w_ref[rows_at(3, k, owned), :] = pieces[4][(k - 1) * owned : k * owned, :]
    else:
        w_ref[...] = pieces[0][...]
        gw_ref = message_refs[0]
    width = bias_up_ref.shape[1]
    heads, out = 3 * BLK, 3 * BLK + width
    slots = keep_ref.shape[0]
    keep, low, high = keep_ref[...], low_ref[...], high_ref[...]

    def turn(x, sign):
        return x * keep + sign * (
            pltpu.roll(x, BLK - ROT // 2, 1) * low + pltpu.roll(x, ROT // 2, 1) * high
        )

    lane = lax.broadcasted_iota(jnp.int32, (slots, BLK), 1)
    first = lane < HD
    q_row = lax.broadcasted_iota(jnp.int32, (2 * slots, slots), 0) & (slots - 1)
    k_row = lax.broadcasted_iota(jnp.int32, (2 * slots, slots), 1)

    def stacked(x):
        zero = jnp.zeros_like(x)
        return jnp.concatenate([jnp.where(first, x, zero), jnp.where(first, zero, x)], axis=0)

    def joined(x):
        return jnp.where(first, x[:slots], x[slots:])

    total = jnp.zeros((1, 3 * BLK), F32)
    total_up = jnp.zeros((1, width), F32)
    for k in range(PLANE):
        at = pl.ds(k * slots, slots)
        proj = dot(x1_ref[at, :], w_ref[:, :heads]) + bias_ref[...]
        hidden = dot(x2_ref[at, :], w_ref[:, heads:out]) + bias_up_ref[...]
        back = dot(g_ref[at, :], w_ref[:, out:])
        query = stacked((turn(proj[:, :BLK], 1.0) * HD**-0.5).astype(BF16))
        key = turn(proj[:, BLK : 2 * BLK], 1.0).astype(BF16)
        value = proj[:, 2 * BLK :].astype(BF16)
        ga = stacked(back[:, :BLK].astype(BF16))
        logits = dot_nt(query, key)
        live = k_row.astype(F32) < length_ref[k : k + 1, 0:1]
        allowed = (k_row <= q_row) & (live | (k_row == q_row))
        logits = jnp.where(allowed, logits, -1000000000.0)
        weights = jnp.exp(logits - jnp.max(logits, axis=-1, keepdims=True))
        probs = weights / jnp.sum(weights, axis=-1, keepdims=True)
        rounded = probs.astype(BF16)
        za_ref[at, :BLK] = joined(dot(rounded, value)).astype(BF16)
        grad_probs = dot_nt(ga, value)
        inner = jnp.sum(probs * grad_probs, axis=-1, keepdims=True)
        grad_logits = (probs * (grad_probs - inner)).astype(BF16)
        grad_query = joined(dot(grad_logits, key)) * HD**-0.5
        grad_key = dot_tn(grad_logits, query)
        grad_value = dot_tn(rounded, ga)
        gp = jnp.concatenate([turn(grad_query, -1.0), turn(grad_key, -1.0), grad_value], axis=1).astype(BF16)
        gp_ref[at, :] = gp
        total = total + jnp.sum(gp.astype(F32), axis=0, keepdims=True)
        part = 0.5 + 0.5 * lax.erf(hidden * (0.5**0.5))
        za_ref[at, BLK:] = (hidden * part).astype(BF16)
        slope = part + hidden * jnp.exp(-0.5 * hidden * hidden) * (2.0 * math.pi) ** -0.5
        gh = (back[:, BLK:] * slope).astype(BF16)
        gh_ref[at, :] = gh
        total_up = total_up + jnp.sum(gh.astype(F32), axis=0, keepdims=True)
    gb_ref[:, :width] = total_up
    gb_ref[:, width:] = total
    gw_ref[:, :heads] = dot_tn(x1_ref[...], gp_ref[...]).astype(BF16)
    gw_ref[:, heads:out] = dot_tn(x2_ref[...], gh_ref[...]).astype(BF16)
    gw_ref[:, out:] = dot_tn(g_ref[...], za_ref[...]).astype(BF16)
    if levels:
        for m in range(levels):
            for k in range(PLANE):
                message_refs[m][k * owned : (k + 1) * owned, :] = gw_ref[rows_at(m, k, owned), :]


def products_kernel(
    params_ref, xh_ref, w_ref, za_ref, gp_ref, gh_ref, gb_ref, bo_ref, keep_ref, send_ref, notes_ref, stage_ref
):
    half = lax.axis_index("tensor")
    slots = stage_ref.shape[1]
    own_rows = slots // 2
    heads, out = 3 * BLK, 3 * BLK + gh_ref.shape[1]
    params = params_ref[...]
    gain1, gain2 = params[0:1], params[2:3]
    sums = [jnp.zeros((1, xh_ref.shape[1]), F32) for _ in range(4)]
    for k in range(PLANE):
        at = pl.ds(k * slots, slots)
        stage_ref[0] = dot_nt(za_ref[at, :], w_ref[:, out:])
        g1 = dot_nt(gp_ref[at, :], w_ref[:, :heads])
        g2 = dot_nt(gh_ref[at, :], w_ref[:, heads:out])
        stage_ref[1] = gain1 * g1 + gain2 * g2
        xh = xh_ref[at, :].astype(F32)
        for j, term in enumerate((g1 * xh, g1, g2 * xh, g2)):
            sums[j] = sums[j] + jnp.sum(term, axis=0, keepdims=True)
        mine = pl.ds(pl.multiple_of(half * own_rows, own_rows), own_rows)
        other = pl.ds(pl.multiple_of((1 - half) * own_rows, own_rows), own_rows)
        for j in range(2):
            to = pl.ds(k * slots + j * own_rows, own_rows)
            keep_ref[to, :] = stage_ref[j, mine, :].astype(BF16)
            send_ref[to, :] = stage_ref[j, other, :].astype(BF16)
    zero = jnp.zeros((NOTES - 6, xh_ref.shape[1]), F32)
    notes_ref[...] = jnp.concatenate([gb_ref[...], bo_ref[...]] + sums + [zero], axis=0).astype(BF16)


def join_kernel(*refs):
    part_refs, (every_ref, others_ref) = refs[:PLANE], refs[PLANE:]
    owned = part_refs[0].shape[0]
    for k, ref in enumerate(part_refs):
        every_ref[k * owned : (k + 1) * owned, :] = ref[...]
        if k:
            others_ref[(k - 1) * owned : k * owned, :] = ref[...]


def choose_kernel(own_ref, own_far_ref, others_ref, far_ref, out_ref):
    owned = own_ref.shape[0]
    for at, mine, afar in ((0, own_ref, own_far_ref), (owned, others_ref, far_ref)):
        rows = pl.ds(at, mine.shape[0])
        out_ref[rows, :] = jnp.where(is_inner(), afar[...].astype(F32), mine[...].astype(F32)).astype(BF16)


def relay_kernel(far_ref, passed_ref, out_ref):
    passed = jnp.where(is_inner(), passed_ref[...].astype(F32), 0.0)
    out_ref[...] = (far_ref[...].astype(F32) + passed).astype(BF16)


def pair_kernel(keep_ref, peer_ref, *refs):
    note_refs, out_refs = refs[:-PLANE], refs[-PLANE:]
    slots = out_refs[0].shape[0] - NOTES
    notes = tree_sum([ref[...].astype(F32) for ref in note_refs]).astype(BF16)
    for k, out_ref in enumerate(out_refs):
        at = pl.ds(k * slots, slots)
        out_ref[:slots, :] = (keep_ref[at, :].astype(F32) + peer_ref[at, :].astype(F32)).astype(BF16)
        out_ref[slots:, :] = notes


def rows_out_kernel(residual_ref, g_ref, b_out_ref, b_down_ref, *refs):
    part_refs, (result_ref, grad_ref, notes_ref) = refs[:PLANE], refs[PLANE:]
    own_rows = residual_ref.shape[0]
    slots = 2 * own_rows
    branch = tree_sum([ref[:own_rows, :].astype(F32) for ref in part_refs])
    x = residual_ref[...].astype(F32)
    result_ref[...] = (x + (branch + b_out_ref[...] + b_down_ref[...])).astype(BF16)
    off = x - jnp.mean(x, axis=-1, keepdims=True)
    scale = lax.rsqrt(jnp.mean(off * off, axis=-1, keepdims=True) + eps)
    xh = off * scale
    grad = tree_sum([ref[own_rows:slots, :].astype(F32) for ref in part_refs])
    grad = grad - jnp.mean(grad, axis=-1, keepdims=True) - xh * jnp.mean(grad * xh, axis=-1, keepdims=True)
    grad_ref[...] = g_ref[...].astype(F32) + scale * grad
    notes = [ref[slots:, :].astype(F32) for ref in part_refs]
    zero = jnp.zeros((NOTES - PLANE - 5, x.shape[1]), F32)
    notes = jnp.concatenate([note[0:1] for note in notes] + [tree_sum(notes)[1:6], zero], axis=0)
    notes_ref[...] = notes


def combine_kernel(own_ref, near_ref, passed_ref, far_ref, *out_refs):
    owned = own_ref.shape[0] // PLANE
    passed_here = jnp.logical_not(is_inner())
    for k, out_ref in enumerate(out_refs):
        at = pl.ds(k * owned, owned)
        total = own_ref[at, :].astype(F32) + near_ref[at, :].astype(F32) + far_ref[at, :].astype(F32)
        total = total + jnp.where(passed_here, passed_ref[at, :].astype(F32), 0.0)
        out_ref[...] = total.astype(out_ref.dtype)


def owner_kernel(*refs):
    part_refs, (notes_ref, peer_notes_ref) = refs[:PLANE], refs[PLANE:-12]
    up_ref, down_ref, qkv_ref, out_ref, b_up_ref, b_qkv_ref = refs[-12:-6]
    common_refs = refs[-6:]
    width = up_ref.shape[1] // PLANE
    head_blocks = out_ref.shape[1] // BLK
    heads, out = 3 * BLK, 3 * BLK + width
    notes = notes_ref[...]
    common = notes + peer_notes_ref[...]
    for k, part_ref in enumerate(part_refs):
        other = place()[0] ^ k
        at = pl.ds(pl.multiple_of(other * width, BLK), width)
        up_ref[:, at] = part_ref[:, heads:out].astype(F32)
        down_ref[:, at] = part_ref[:, out + BLK :].astype(F32)
        for j in range(width // BLK):
            b_up_ref[pl.ds(other * (width // BLK) + j, 1), :] = notes[k : k + 1, j * BLK : (j + 1) * BLK]

        @pl.when(other < head_blocks)
        def _():
            at = pl.ds(pl.multiple_of(other * BLK, BLK), BLK)
            for c in range(3):
                qkv_ref[c, :, at] = part_ref[:, c * BLK : (c + 1) * BLK].astype(F32)
                b_qkv_ref[c : c + 1, at] = notes[k : k + 1, width + c * BLK : width + (c + 1) * BLK]
            out_ref[:, at] = part_ref[:, out : out + BLK].astype(F32)

    for row, common_ref in zip((0, 0, 1, 2, 3, 4), common_refs):
        row = PLANE + row
        for j in range(common_ref.shape[0]):
            common_ref[j : j + 1, :] = common[row : row + 1, j * BLK : (j + 1) * BLK]


def kernel_call(body, out_shapes, operands, scratch=(), micros=1.0, space=pltpu.VMEM, limit=20):
    vmem = pl.BlockSpec(memory_space=pltpu.VMEM)
    taken = pl.BlockSpec(memory_space=space)
    return pl.pallas_call(
        body,
        out_shape=out_shapes,
        in_specs=[taken] * len(operands),
        out_specs=[vmem] * len(out_shapes),
        scratch_shapes=list(scratch),
        compiler_params=pltpu.CompilerParams(vmem_limit_bytes=limit * 2**20),
        cost_estimate=pl.CostEstimate(flops=int(micros * 1e9), bytes_accessed=1, transcendentals=0),
    )(*operands)


def per_device(
    residual,
    cotangent,
    seq_lengths,
    gain_attn,
    shift_attn,
    gain_mlp,
    shift_mlp,
    w_qkv,
    b_qkv,
    w_out,
    b_out,
    w_up,
    b_up,
    w_down,
    b_down,
):
    places = lax.axis_size("dp")
    levels = places // PLANE
    plane_at = place()[0]
    own_rows, model = residual.shape
    slots = 2 * own_rows
    rows_all = PLANE * slots
    owned = w_up.shape[0]
    width = w_up.shape[1] // PLANE
    head_blocks = w_out.shape[0] // BLK
    columns = 4 * BLK + 2 * width
    direct = levels if levels == 4 and owned % 16 == 0 else 0
    level_groups = [[lev * PLANE + j for lev in range(levels)] for j in range(PLANE)]
    shape = jax.ShapeDtypeStruct

    def to_plane(x, k):
        return lax.ppermute(x, "dp", [(j, j ^ k) for j in range(places)])

    def to_level(x, m):
        return lax.ppermute(x, "dp", [(j, j ^ (m * PLANE)) for j in range(places)])

    def to_peer(x):
        return lax.ppermute(x, "tensor", [(0, 1), (1, 0)])

    passing = [(0, 2), (3, 1), (1, 0), (2, 3)]

    def to_pass(x, back=False):
        pairs = [(b, a) if back else (a, b) for a, b in passing]
        return lax.ppermute(x, "dp", [(a * PLANE + j, b * PLANE + j) for a, b in pairs for j in range(PLANE)])

    held = (w_qkv, w_out.T, w_up, w_down.T)
    shares = kernel_call(
        share_kernel,
        [shape((owned, columns), BF16)] * PLANE,
        held,
        scratch=[pltpu.VMEM(a.shape, a.dtype) for a in held] + [pltpu.SemaphoreType.DMA((4,))],
        space=pl.ANY,
        limit=63,
    )
    received = [to_plane(shares[k], k) for k in range(1, PLANE)]
    residual_m, cotangent_m, lengths_m, _ = lax.optimization_barrier((residual, cotangent, seq_lengths, shares))
    row = lax.axis_index("tensor") * own_rows + jnp.arange(own_rows, dtype=jnp.int32)
    live = (row < jnp.sum(lengths_m[0]))[:, None]
    message = jnp.concatenate([residual_m, jnp.where(live, cotangent_m, jnp.asarray(MARK, BF16))], axis=0)
    if direct:
        own = shares[0]
        own_far = to_level(own, 3)
        every, others = kernel_call(
            join_kernel,
            [shape((PLANE * owned, columns), BF16), shape(((PLANE - 1) * owned, columns), BF16)],
            (own, *received),
            micros=20,
        )
        every, others, message = lax.optimization_barrier((every, others, message))
        near, far = to_level(every, 1), to_level(others, 3)
        near, far = lax.optimization_barrier((near, far))
        message, own_far = lax.optimization_barrier((message, own_far))
        chosen = kernel_call(
            choose_kernel,
            [shape((PLANE * owned, columns), BF16)],
            (own, own_far, others, far),
            micros=20,
        )[0]
    messages = [message] + [to_plane(message, k) for k in range(1, PLANE)]
    if direct:
        pieces = [every, near, to_pass(chosen), own_far, far]
    else:
        every = jnp.concatenate(xor_sorted([shares[0]] + received, plane_at), axis=0)
        pieces = [lax.all_gather(every, "dp", axis=0, tiled=True, axis_index_groups=level_groups)]
    rows = jnp.concatenate(messages, axis=0)
    params = jnp.stack([gain_attn, shift_attn, gain_mlp, shift_mlp] + [jnp.zeros_like(gain_attn)] * 4)
    x1, x2, xh, g, g_own, lengths, bo = kernel_call(
        rows_kernel,
        [shape((rows_all, model), BF16)] * 4
        + [shape((own_rows, model), BF16), shape((8, 128), F32), shape((1, model), F32)],
        (params, rows, to_peer(rows)),
        micros=1,
    )

    block_at = jnp.minimum(plane_at, head_blocks - 1) * BLK
    bias_heads = lax.dynamic_slice_in_dim(b_qkv, block_at, BLK, 1).reshape(1, 3 * BLK)
    bias_up = lax.dynamic_slice_in_dim(b_up, plane_at * width, width, 0).reshape(1, width)
    za, gp, gh, w, gb, *messages = kernel_call(
        partial(layer_kernel, direct),
        [
            shape((rows_all, BLK + width), BF16),
            shape((rows_all, 3 * BLK), BF16),
            shape((rows_all, width), BF16),
            shape((model, columns), BF16),
            shape((1, width + 3 * BLK), F32),
        ]
        + [shape((PLANE * owned if direct else model, columns), BF16)] * max(direct, 1),
        (lengths, x1, x2, g, bias_heads, bias_up, *rotary_tables(slots), *pieces),
        scratch=[pltpu.VMEM((model, columns), BF16)],
        micros=12,
        limit=30,
    )
    if direct:
        passed = to_pass(messages[2], back=True)
    keep, send, notes = kernel_call(
        products_kernel,
        [shape((rows_all, model), BF16)] * 2 + [shape((NOTES, model), BF16)],
        (params, xh, w, za, gp, gh, gb, bo),
        scratch=[pltpu.VMEM((2, slots, model), F32)],
        micros=4,
    )
    from_peer = to_peer(send)
    if direct:
        notes = (notes.astype(F32) + to_level(notes, 1).astype(F32)).astype(BF16)
        notes = [notes, to_level(notes, 2)]
        relayed = kernel_call(
            relay_kernel, [shape((PLANE * owned, columns), BF16)], (messages[3], passed), micros=20
        )[0]
        relayed, keep, messages = lax.optimization_barrier((relayed, keep, messages))
    else:
        notes = lax.all_gather(notes, "dp", axis=0, axis_index_groups=level_groups)
        notes = [jnp.sum(notes.astype(F32), axis=0)]
    outgoing = kernel_call(
        pair_kernel,
        [shape((slots + NOTES, model), BF16)] * PLANE,
        (keep, from_peer, *notes),
        micros=2,
    )
    parts = [outgoing[0]] + [to_plane(outgoing[k], k) for k in range(1, PLANE)]

    if direct:
        near, far = to_level(messages[1], 1), to_level(relayed, 3)
        parts, near, far = lax.optimization_barrier((parts, near, far))
        backs = kernel_call(
            combine_kernel,
            [shape((owned, columns), F32)] + [shape((owned, columns), BF16)] * (PLANE - 1),
            (messages[0], near, passed, far),
        )
    else:
        sums = lax.psum_scatter(
            messages[0], "dp", scatter_dimension=0, tiled=True, axis_index_groups=level_groups
        ).reshape(PLANE, owned, columns)
        backs = [lax.dynamic_index_in_dim(sums, plane_at ^ k, 0, keepdims=False) for k in range(PLANE)]
    backs = [backs[0]] + [to_plane(backs[k], k) for k in range(1, PLANE)]
    result, grad_residual, notes = kernel_call(
        rows_out_kernel,
        [shape((own_rows, model), BF16), shape((own_rows, model), F32), shape((NOTES, model), F32)],
        (residual, g_own, b_out.reshape(1, model), b_down.reshape(1, model), *parts),
    )
    grad_up, grad_down, grad_qkv, grad_out_w, grad_b_up, grad_b_qkv, *common = kernel_call(
        owner_kernel,
        [
            shape((owned, PLANE * width), F32),
            shape((owned, PLANE * width), F32),
            shape((3, owned, head_blocks * BLK), F32),
            shape((owned, head_blocks * BLK), F32),
            shape((PLANE * width // BLK, BLK), F32),
            shape((3, head_blocks * BLK), F32),
        ]
        + [shape((model // BLK, BLK), F32)] * 6,
        (*backs, notes, to_peer(notes)),
    )
    common = [total.reshape(model) for total in common]
    return (
        result,
        grad_residual,
        *common[2:],
        grad_qkv,
        grad_b_qkv,
        grad_out_w.T,
        common[0],
        grad_up,
        grad_b_up.reshape(PLANE * width),
        grad_down.T,
        common[1],
    )


def solution(mesh):
    return jax.shard_map(
        per_device,
        mesh=mesh,
        in_specs=(
            P(("dp", "tensor"), None),
            P(("dp", "tensor"), None),
            P("dp", None),
            P(),
            P(),
            P(),
            P(),
            P(None, "dp", "tensor"),
            P(None, "tensor"),
            P("tensor", "dp"),
            P(),
            P("dp", "tensor"),
            P("tensor"),
            P("tensor", "dp"),
            P(),
        ),
        out_specs=(
            P(("dp", "tensor"), None),
            P(("dp", "tensor"), None),
            P(),
            P(),
            P(),
            P(),
            P(None, "dp", "tensor"),
            P(None, "tensor"),
            P("tensor", "dp"),
            P(),
            P("dp", "tensor"),
            P("tensor"),
            P("tensor", "dp"),
            P(),
        ),
        check_vma=False,
    )
```
